32 devices in a mesh: grp: 8 (over y, x, core), dp: 4 (over z).
Axes of the slice: x: 2, y: 2, z: 4, core: 2. Of those that a mesh axis runs over, the one named last changes fastest.
Arguments:
- tokens: bfloat16 [32, 1024, 1024], P(('grp', 'dp')), may hold values from -6 to 6
- out_cotangent: bfloat16 [32, 1024, 1024], P(('grp', 'dp')), may hold values from -6 to 6
- lengths: int32 [32], replicated, may hold values from 256 to 1024, as said below
- places: int32 [32, 64], replicated, may hold values from 0 to 255, as said below
- deal: int32 [32], replicated, may hold values from 0 to 31, each once
- in_weights: float32 [6, 1024, 1024], P(None, 'grp', 'dp'), may hold values from -0.1875 to 0.1875
- out_weight: float32 [1024, 1024], P('grp', 'dp'), may hold values from -4 to 4
- up_weight: float32 [1024, 4096], P('grp', 'dp'), may hold values from -0.1875 to 0.1875
- down_weight: float32 [4096, 1024], P('grp', 'dp'), may hold values from -0.09375 to 0.09375
- vectors: float32 [14, 1024], P(None, 'dp')
- first_in: float32 [6, 1024, 1024], P(None, 'grp', 'dp'), may hold values from -6 to 6
- first_out: float32 [1024, 1024], P('grp', 'dp'), may hold values from -6 to 6
- first_up: float32 [1024, 4096], P('grp', 'dp'), may hold values from -6 to 6
- first_down: float32 [4096, 1024], P('grp', 'dp'), may hold values from -6 to 6
- first_vectors: float32 [14, 1024], P(None, 'dp'), may hold values from -180 to 180
- second_in: float32 [6, 1024, 1024], P(None, 'grp', 'dp'), may hold values from 1 to 100
- second_out: float32 [1024, 1024], P('grp', 'dp'), may hold values from 0.01 to 1
- second_up: float32 [1024, 4096], P('grp', 'dp'), may hold values from 1 to 100
- second_down: float32 [4096, 1024], P('grp', 'dp'), may hold values from 1 to 100
- second_vectors: float32 [14, 1024], P(None, 'dp'), may hold values from 1 to 100
Outputs:
- layer_out: bfloat16 [32, 1024, 1024], P(('grp', 'dp'))
- token_gradient: bfloat16 [32, 1024, 1024], P(('grp', 'dp'))
- update_in: float32 [6, 1024, 1024], P(None, 'grp', 'dp')
- update_out: float32 [1024, 1024], P('grp', 'dp')
- update_up: float32 [1024, 4096], P('grp', 'dp')
- update_down: float32 [4096, 1024], P('grp', 'dp')
- update_vectors: float32 [14, 1024], P(None, 'dp')
- moment_in: float32 [6, 1024, 1024], P(None, 'grp', 'dp')
- moment_out: float32 [1024, 1024], P('grp', 'dp')
- moment_up: float32 [1024, 4096], P('grp', 'dp')
- moment_down: float32 [4096, 1024], P('grp', 'dp')
- moment_vectors: float32 [14, 1024], P(None, 'dp')
- square_in: float32 [6, 1024, 1024], P(None, 'grp', 'dp')
- square_out: float32 [1024, 1024], P('grp', 'dp')
- square_up: float32 [1024, 4096], P('grp', 'dp')
- square_down: float32 [4096, 1024], P('grp', 'dp')
- square_vectors: float32 [14, 1024], P(None, 'dp')
The draws below stay inside these ranges and needn't reach their ends.
Inputs may be any that keep to these rules, and one draw needn't show every extreme that they name: `lengths`: one sequence has exactly 1024 tokens; every length is 256 or more. `places`: each row holds 64 distinct increasing positions below 256, hence below that sequence's length. Sequence s is computed by the device of index deal[s] along grp+dp.
All inputs are finite; a program needn't handle non-finite values.
Results may differ from the reference program's by a relative error of at most 0.02.
Values may be sent and summed in bfloat16 or wider, within the bound.
A program may use at most 448 MiB of HBM per device.

```python
import math
import jax
import jax.numpy as jnp
from jax import lax

D = 1024
H = 16
HD = 64
FF = 4096
W = 512
NG = 64
LMAX = 1024
STEP = 10
NV = 14
SEQS = 32


def draw_lengths(key, part):
    key = jax.random.fold_in(key, 11)
    key_drawn, key_chosen = jax.random.split(key)
    drawn = jax.random.randint(key_drawn, (SEQS,), LMAX // 4, LMAX + 1)
    chosen = jax.random.randint(key_chosen, (), 0, SEQS)
    return jnp.where(jnp.arange(SEQS) == chosen, LMAX, drawn).astype(jnp.int32)


def draw_places(key, part):
    key = jax.random.fold_in(key, 12)
    bound_top = LMAX // 4
    scores = jax.random.randint(key, (SEQS, bound_top), 0, 1 << 20) * bound_top + jnp.arange(bound_top)[None, :]
    ranked = jnp.argsort(scores, axis=1)[:, :NG]
    return jnp.sort(ranked, axis=1).astype(jnp.int32)


def draw_vectors(key, part):
    key = jax.random.fold_in(key, 13)
    key_offset, key_scale = jax.random.split(key)
    offsets = 0.2 * jax.random.normal(key_offset, (NV, D), jnp.float32)
    scales = jax.random.uniform(key_scale, (NV, D), jnp.float32, 0.5, 1.5)
    row_index = jnp.arange(NV)[:, None]
    chosen = (row_index == NV - 4) | (row_index == NV - 2)
    return jnp.where(chosen, scales, offsets)


def levels(key, shape, cuts, least, high):
    factor_of = 1.0
    for axis_at, shards_of in cuts:
        draws = jax.random.uniform(jax.random.fold_in(jax.random.fold_in(key, 6), axis_at), (shards_of,), jnp.float32, least / len(cuts), high / len(cuts))
        factor_of = factor_of * jnp.repeat(jnp.exp(draws), shape[axis_at] // shards_of).reshape((-1,) + (1,) * (len(shape) - 1 - axis_at))
    return factor_of


def normal_values(own_key, shape, deviation, limit, cuts=(), kind=jnp.bfloat16):
    entries = deviation * jax.random.normal(own_key, shape, jnp.float32)
    if cuts:
        entries = entries * levels(own_key, shape, cuts, -0.22, 0.18)
    return jnp.clip(entries, -limit, limit).astype(kind)


def setup_inputs(seed: int = 0) -> dict:
    key_list = jax.random.split(jax.random.key(seed), 21)
    return {
        "tokens": normal_values(key_list[0], (SEQS, LMAX, D), 1.0, 6.0, ((0, 32),)),
        "out_cotangent": normal_values(key_list[1], (SEQS, LMAX, D), 1.0, 6.0, ((0, 32),)),
        "lengths": draw_lengths(jax.random.fold_in(key_list[20], 71), 0),
        "places": draw_places(jax.random.fold_in(key_list[20], 71), 0),
        "deal": jax.random.permutation(key_list[4], SEQS).astype(jnp.int32),
        "in_weights": normal_values(key_list[5], (6, D, D), D ** -0.5, 0.1875, ((1, 8), (2, 4)), jnp.float32),
        "out_weight": normal_values(key_list[6], (D, D), (max(D // W, 1)) ** -0.5, 4.0, ((0, 8), (1, 4)), jnp.float32),
        "up_weight": normal_values(key_list[7], (D, FF), D ** -0.5, 0.1875, ((0, 8), (1, 4)), jnp.float32),
        "down_weight": normal_values(key_list[8], (FF, D), FF ** -0.5, 0.09375, ((0, 8), (1, 4)), jnp.float32),
        "vectors": draw_vectors(jax.random.fold_in(key_list[20], 71), 0),
        "first_in": normal_values(key_list[10], (6, D, D), 1.0, 6.0, ((1, 8), (2, 4)), jnp.float32),
        "first_out": normal_values(key_list[11], (D, D), 1.0, 6.0, ((0, 8), (1, 4)), jnp.float32),
        "first_up": normal_values(key_list[12], (D, FF), 1.0, 6.0, ((0, 8), (1, 4)), jnp.float32),
        "first_down": normal_values(key_list[13], (FF, D), 1.0, 6.0, ((0, 8), (1, 4)), jnp.float32),
        "first_vectors": normal_values(key_list[14], (NV, D), 30.0, 180.0, ((1, 4),), jnp.float32),
        "second_in": jnp.clip(jnp.exp(math.log(100.0) - 4.6051702 * jax.random.uniform(key_list[15], (6, D, D), jnp.float32) ** levels(key_list[15], (6, D, D), ((1, 8), (2, 4)), -0.2, 0.2)), 1.0, 100.0),
        "second_out": jnp.clip(jnp.exp(math.log(1.0) - 4.6051702 * jax.random.uniform(key_list[16], (D, D), jnp.float32) ** levels(key_list[16], (D, D), ((0, 8), (1, 4)), -0.2, 0.2)), 0.01, 1.0),
        "second_up": jnp.clip(jnp.exp(math.log(100.0) - 4.6051702 * jax.random.uniform(key_list[17], (D, FF), jnp.float32) ** levels(key_list[17], (D, FF), ((0, 8), (1, 4)), -0.2, 0.2)), 1.0, 100.0),
        "second_down": jnp.clip(jnp.exp(math.log(100.0) - 4.6051702 * jax.random.uniform(key_list[18], (FF, D), jnp.float32) ** levels(key_list[18], (FF, D), ((0, 8), (1, 4)), -0.2, 0.2)), 1.0, 100.0),
        "second_vectors": jnp.clip(jnp.exp(math.log(100.0) - 4.6051702 * jax.random.uniform(key_list[19], (NV, D), jnp.float32) ** levels(key_list[19], (NV, D), ((1, 4),), -0.2, 0.2)), 1.0, 100.0),
    }


EPS_NORM = 1e-05
WEIGHT_DECAY = 0.1
BETA_FIRST = 0.5
BETA_SECOND = 0.999
EPS_ADAM = 1e-08
NEGATIVE = -1e+30

@jax.custom_vjp
def low(v):
    return lax.optimization_barrier(v.astype(jnp.bfloat16)).astype(jnp.float32)

@jax.custom_vjp
def low_back(v):
    return v

def low_keep(v):
    return (low(v), None)

def low_pass(kept, grad):
    return (grad,)

def back_keep(v):
    return (v, None)

def back_low(kept, grad):
    return (low(grad),)
low.defvjp(low_keep, low_pass)
low_back.defvjp(back_keep, back_low)

def rounded(values):
    return low_back(low(values))

def matmul(left_side, right_side):
    return jnp.dot(left_side, right_side, precision=lax.Precision.HIGHEST, preferred_element_type=jnp.float32)

def einsum_high(pattern, left_side, right_side):
    return jnp.einsum(pattern, left_side, right_side, precision=lax.Precision.HIGHEST, preferred_element_type=jnp.float32)

def norm_rows(mixture):
    centered = mixture - lax.optimization_barrier(jnp.mean(mixture, axis=-1, keepdims=True))
    variance = lax.optimization_barrier(jnp.mean(centered * centered, axis=-1, keepdims=True))
    return centered * lax.rsqrt(variance + EPS_NORM)

def split_heads(matrix):
    return matrix.reshape(matrix.shape[0], H, HD)

def masked_softmax(scores, allowed):
    return jax.nn.softmax(jnp.where(allowed, scores, NEGATIVE), axis=-1)

def one_sequence(params, sequence, length, spots):
    in_weights, out_weight, up_weight, down_weight, vectors = params
    extra = FF // D
    span = sequence.shape[0]
    positions = jnp.arange(span, dtype=jnp.int32)
    global_row = jnp.any(positions[:, None] == spots[None, :], axis=1)
    key_valid = positions < length
    scale = HD ** (-0.5)
    query = rounded(matmul(sequence, in_weights[0]) + vectors[0])
    keys_local = rounded(matmul(sequence, in_weights[1]))
    values_local = rounded(matmul(sequence, in_weights[2]) + vectors[1])
    query_global = rounded(matmul(sequence[spots], in_weights[3]) + vectors[3])
    keys_global = rounded(matmul(sequence, in_weights[4]))
    values_global = rounded(matmul(sequence, in_weights[5]) + vectors[4])
    scores = low_back(einsum_high('ihd,jhd->hij', split_heads(query), split_heads(keys_local)) * scale)
    near = jnp.abs(positions[:, None] - positions[None, :]) <= W // 2
    allowed = (near | global_row[None, :]) & key_valid[None, :]
    local_weights = low(masked_softmax(scores, allowed[None]))
    local_out = einsum_high('hij,jhd->ihd', local_weights, split_heads(values_local)).reshape(span, D)
    global_scores = low_back(einsum_high('ghd,jhd->hgj', split_heads(query_global), split_heads(keys_global)) * scale)
    global_weights = low(masked_softmax(global_scores, key_valid[None, None, :]))
    global_out = einsum_high('hgj,jhd->ghd', global_weights, split_heads(values_global)).reshape(NG, D)
    attended = rounded(local_out.at[spots].set(global_out))
    branch = low_back(matmul(attended, out_weight) + vectors[2])
    first_norm = norm_rows(sequence + branch) * vectors[6 + extra] + vectors[7 + extra]
    hidden_pre = low_back(matmul(low(first_norm), up_weight) + vectors[5:5 + extra].reshape(-1))
    hidden_act = low(jax.nn.gelu(hidden_pre, approximate=False))
    feed_out = low_back(matmul(hidden_act, down_weight) + vectors[5 + extra])
    result = norm_rows(first_norm + feed_out) * vectors[8 + extra] + vectors[9 + extra]
    return result * key_valid[:, None].astype(jnp.float32)

def adam_update(weight, gradient, moment, square, decay_rate, fix_first, fix_second):
    moment_new = BETA_FIRST * moment + (1.0 - BETA_FIRST) * gradient
    square_new = BETA_SECOND * square + (1.0 - BETA_SECOND) * gradient * gradient
    update = moment_new / fix_first / (jnp.sqrt(square_new / fix_second) + EPS_ADAM)
    return (update + decay_rate * weight, moment_new, square_new)

def reference(tokens, out_cotangent, lengths, places, deal, in_weights, out_weight, up_weight, down_weight, vectors, first_in, first_out, first_up, first_down, first_vectors, second_in, second_out, second_up, second_down, second_vectors):
    inverse = jnp.argsort(deal).astype(jnp.int32)
    params = (in_weights, out_weight, up_weight, down_weight, vectors)

    def forward(weights, inputs):
        lowered = jax.tree.map(low, weights)

        def per_sequence(bundle):
            return one_sequence(lowered, bundle[0], bundle[1], bundle[2])
        return lax.map(jax.checkpoint(per_sequence), (inputs[inverse], lengths[inverse], places[inverse]))
    outputs, pullback = jax.vjp(forward, params, tokens.astype(jnp.float32))
    weight_grads, token_grads = pullback(out_cotangent.astype(jnp.float32))
    grad_in, grad_out, grad_up, grad_down, grad_vectors = weight_grads
    step_count = jnp.float32(STEP)
    fix_first = 1.0 - jnp.power(jnp.float32(BETA_FIRST), step_count)
    fix_second = 1.0 - jnp.power(jnp.float32(BETA_SECOND), step_count)
    update_in, moment_in, square_in = adam_update(in_weights, grad_in, first_in, second_in, WEIGHT_DECAY, fix_first, fix_second)
    update_out, moment_out, square_out = adam_update(out_weight, grad_out, first_out, second_out, WEIGHT_DECAY, fix_first, fix_second)
    update_up, moment_up, square_up = adam_update(up_weight, grad_up, first_up, second_up, WEIGHT_DECAY, fix_first, fix_second)
    update_down, moment_down, square_down = adam_update(down_weight, grad_down, first_down, second_down, WEIGHT_DECAY, fix_first, fix_second)
    update_vectors, moment_vectors, square_vectors = adam_update(vectors, grad_vectors, first_vectors, second_vectors, 0.0, fix_first, fix_second)
    return (outputs.astype(jnp.bfloat16), token_grads.astype(jnp.bfloat16), update_in, update_out, update_up, update_down, update_vectors, moment_in, moment_out, moment_up, moment_down, moment_vectors, square_in, square_out, square_up, square_down, square_vectors)
```

```python
import jax
import jax.numpy as jnp
import numpy as np
from jax import lax
from jax.experimental import pallas as pl
from jax.experimental.pallas import tpu as pltpu
from jax.sharding import PartitionSpec as P

D = 1024
H = 16
HD = 64
FF = 4096
W = 512
NG = 64
STEP = 10

EPS_NORM = 1e-05
WEIGHT_DECAY = 0.1
BETA_FIRST = 0.5
BETA_SECOND = 0.999
EPS_ADAM = 1e-08
NEGATIVE = -1e30

MESH = pl.DeviceIdType.MESH
MIB = 1 << 20
BF = jnp.bfloat16
F32 = jnp.float32
LANES = 128
ROWS = 256
ANYSPEC = pl.BlockSpec(memory_space=pl.ANY)
VMEMSPEC = pl.BlockSpec(memory_space=pltpu.VMEM)


def product(left_side, right_side):
    return jnp.dot(left_side, right_side, preferred_element_type=F32)


def product_back(left_side, right_side):
    return lax.dot_general(
        left_side, right_side, (((1,), (1,)), ((), ())), preferred_element_type=F32
    )


def product_left(left_side, right_side):
    return lax.dot_general(
        left_side, right_side, (((0,), (0,)), ((), ())), preferred_element_type=F32
    )


def column_sums(matrix):
    return jnp.sum(matrix.astype(F32), axis=0)


def adam_update(weight, gradient, moment, square, decay_rate, fix_first, fix_second):
    moment_new = BETA_FIRST * moment + (1.0 - BETA_FIRST) * gradient
    square_new = BETA_SECOND * square + (1.0 - BETA_SECOND) * gradient * gradient
    update = moment_new / fix_first / (jnp.sqrt(square_new / fix_second) + EPS_ADAM)
    return (update + decay_rate * weight, moment_new, square_new)


class Spot:
    def __init__(self, groups, depth):
        self.nb = groups // 4
        self.nz = depth
        self.groups = groups
        g = lax.axis_index("grp")
        self.g = g
        self.z = lax.axis_index("dp")
        self.c = lax.rem(g, 2)
        self.b = lax.rem(lax.div(g, 2), self.nb)
        self.a = lax.div(g, 2 * self.nb)

    def at(self, a=None, b=None, c=None, z=None):
        a = self.a if a is None else a
        b = self.b if b is None else b
        c = self.c if c is None else c
        z = self.z if z is None else z
        return ((a * self.nb + b) * 2 + c, z)

    def b_off(self, i):
        return lax.rem(self.b + i, self.nb)

    def z_off(self, i):
        return lax.rem(self.z + i, self.nz)

    def neighbours(self):
        out = [self.at(a=1 - self.a), self.at(c=1 - self.c)]
        out += [self.at(b=self.b_off(i)) for i in range(1, self.nb)]
        out += [self.at(z=self.z_off(i)) for i in range(1, self.nz)]
        return out


def greet(targets):
    barrier = pltpu.get_barrier_semaphore()
    for target in targets:
        pl.semaphore_signal(barrier, inc=1, device_id=target, device_id_type=MESH)
    pl.semaphore_wait(barrier, len(targets))


class Sems:
    def __init__(self, send, recv):
        self.send, self.recv, self.used = send, recv, 0

    def copy(self, src, dst, target):
        i = self.used
        self.used += 1
        return pltpu.make_async_remote_copy(
            src_ref=src,
            dst_ref=dst,
            send_sem=self.send.at[i],
            recv_sem=self.recv.at[i],
            device_id=target,
            device_id_type=MESH,
        )


def start_all(copies):
    for copy in copies:
        copy.start()


def recv_all(copies):
    for copy in copies:
        copy.wait_recv()


def send_done(copies):
    for copy in copies:
        copy.wait_send()


def gather_copies(nb, nz):
    return (nz - 1) + 1 + (nb - 1) + (nb - 1) + 1 + 1


class GatherPiece:
    def __init__(self, spot, sems, local_sem, src, out):
        a, b, c, z = spot.a, spot.b, spot.c, spot.z
        rows, width = src.shape
        half = rows // 2
        own = pl.ds(pl.multiple_of(z * width, LANES), width)
        top, low = pl.ds(0, half), pl.ds(half, half)
        shard = src
        mine = out.at[a, b, c, :, own]
        self.local = pltpu.make_async_copy(shard, mine, local_sem)
        self.phases = [
            [sems.copy(shard, mine, spot.at(z=spot.z_off(i))) for i in range(1, spot.nz)],
            [sems.copy(out.at[a, b, c, top], out.at[a, b, c, top], spot.at(a=1 - a))]
            + [
                sems.copy(out.at[a, b, c, low], out.at[a, b, c, low], spot.at(b=spot.b_off(i)))
                for i in range(1, spot.nb)
            ],
            [
                sems.copy(out.at[:, b, c, top], out.at[:, b, c, top], spot.at(b=spot.b_off(i)))
                for i in range(1, spot.nb)
            ]
            + [sems.copy(out.at[a, :, c, low], out.at[a, :, c, low], spot.at(a=1 - a))],
            [sems.copy(out.at[:, :, c], out.at[:, :, c], spot.at(c=1 - c))],
        ]

    def start(self, p):
        if p == 0:
            self.local.start()
        if p == 1:
            self.local.wait()
        start_all(self.phases[p])

    def arrive(self, p):
        recv_all(self.phases[p])

    def close(self):
        for phase in self.phases:
            send_done(phase)


class Swap:
    def __init__(self, spot, sems, local_sem, src, dst):
        devices = spot.groups * spot.nz
        me = spot.g * spot.nz + spot.z
        self.local = pltpu.make_async_copy(src.at[me], dst.at[me], local_sem)
        self.copies = []
        for i in range(1, devices):
            other = lax.rem(me + i, devices)
            self.copies.append(
                sems.copy(src.at[other], dst.at[me], (lax.div(other, spot.nz), lax.rem(other, spot.nz)))
            )

    def start(self, part, parts):
        if part == 0:
            self.local.start()
        n = len(self.copies)
        start_all(self.copies[part * n // parts : (part + 1) * n // parts])

    def finish(self):
        self.local.wait()
        recv_all(self.copies)
        send_done(self.copies)


def timeline(pieces, times, which=(0, 1, 2, 3, 4)):
    phases = len(pieces[0].phases)
    steps = {}
    for t in reversed(range(len(pieces))):
        for p in which:
            steps.setdefault(times[t][p], []).append((t, p))

    def run(events):
        for t, p in events:
            if p > 0:
                pieces[t].arrive(p - 1)
            if p < phases:
                pieces[t].start(p)
            else:
                pieces[t].close()

    return {s: (lambda events=events: run(events)) for s, events in steps.items()}


class Ticks:
    def __init__(self, per):
        self.per, self.actions = per, {}

    def add(self, tick, action):
        self.actions.setdefault(tick, []).append(action)

    def add_all(self, actions):
        for tick, action in actions.items():
            self.add(tick, action)

    def here(self, c, first, last):
        for tick in sorted(self.actions):
            if tick % self.per == c and first <= tick // self.per <= last:

                @pl.when(pl.program_id(0) == tick // self.per)
                def _(mine=self.actions[tick]):
                    for action in mine:
                        action()


def during(first, last):
    return pl.when(jnp.logical_and(pl.program_id(0) >= first, pl.program_id(0) <= last))


def in_chunks(span, body):
    def step(i, carry):
        body(pl.ds(pl.multiple_of(i * ROWS, ROWS), ROWS))
        return carry

    lax.fori_loop(0, span // ROWS, step, 0)


def slot_times(slot, count):
    return [
        [0 if t == 0 else slot(t - 1) + 1, slot(t), slot(t + 1) + 1, slot(t + 2) + 2, slot(t + 3) + 3]
        for t in range(count)
    ]


def reduce_copies(nb, nz):
    return 1 + (nb - 1) + 1 + 1 + (nb - 1) + (nz - 1)


class ReducePiece:
    def __init__(self, spot, sems, local_sem, src, width, boxes, finish):
        self.spot, self.finish, self.width = spot, finish, width
        tile, self.r0, self.r1b, self.r1a, self.r2a, self.r2b, self.r3 = boxes
        a, b, c, z = spot.a, spot.b, spot.c, spot.z
        self.acc = acc = tile.at[:, :, c] if src is None else tile.at[:, :, 0]
        other = (tile if src is None else src).at[:, :, 1 - c]
        half = tile.shape[-2] // 2
        self.half = half
        top, low = pl.ds(0, half), pl.ds(half, half)
        self.local = None if src is None else pltpu.make_async_copy(src.at[:, :, c], acc, local_sem)
        columns = lambda zz: pl.ds(pl.multiple_of(zz * self.width, LANES), self.width)
        self.own_columns = columns(z)
        self.phases = [
            [sems.copy(other, self.r0, spot.at(c=1 - c))],
            [
                sems.copy(acc.at[:, spot.b_off(i), top], self.r1b.at[i - 1], spot.at(b=spot.b_off(i)))
                for i in range(1, spot.nb)
            ]
            + [sems.copy(acc.at[1 - a, :, low], self.r1a, spot.at(a=1 - a))],
            [sems.copy(acc.at[1 - a, b, top], self.r2a, spot.at(a=1 - a))]
            + [
                sems.copy(acc.at[a, spot.b_off(i), low], self.r2b.at[i - 1], spot.at(b=spot.b_off(i)))
                for i in range(1, spot.nb)
            ],
            [
                sems.copy(
                    acc.at[a, b, :, columns(spot.z_off(i))], self.r3.at[i - 1], spot.at(z=spot.z_off(i))
                )
                for i in range(1, spot.nz)
            ],
        ]

    def start(self, p):
        if p == 0 and self.local is not None:
            self.local.start()
        start_all(self.phases[p])

    def arrive(self, p):
        spot, acc = self.spot, self.acc
        a, b = spot.a, spot.b
        top, low = pl.ds(0, self.half), pl.ds(self.half, self.half)
        recv_all(self.phases[p])
        if p == 0:
            if self.local is not None:
                self.local.wait()
            for i in range(2):
                for j in range(spot.nb):
                    acc[i, j] = (acc[i, j].astype(F32) + self.r0[i, j].astype(F32)).astype(BF)
        if p == 1:
            for i in range(2):
                total = acc[i, b, top].astype(F32)
                for k in range(spot.nb - 1):
                    total = total + self.r1b[k, i].astype(F32)
                acc[i, b, top] = total.astype(BF)
            for j in range(spot.nb):
                acc[a, j, low] = (acc[a, j, low].astype(F32) + self.r1a[j].astype(F32)).astype(BF)
        if p == 2:
            acc[a, b, top] = (acc[a, b, top].astype(F32) + self.r2a[...].astype(F32)).astype(BF)
            total = acc[a, b, low].astype(F32)
            for k in range(spot.nb - 1):
                total = total + self.r2b[k].astype(F32)
            acc[a, b, low] = total.astype(BF)
        if p == 3:
            total = acc[a, b, :, self.own_columns].astype(F32)
            for k in range(spot.nz - 1):
                total = total + self.r3[k].astype(F32)
            self.finish(total)

    def close(self):
        for phase in self.phases:
            send_done(phase)


def reduce_boxes(nb, nz, rows, columns):
    half = rows // 2
    return [
        pltpu.VMEM((2, nb, 2, rows, columns), BF),
        pltpu.VMEM((2, nb, rows, columns), BF),
        pltpu.VMEM((nb - 1, 2, half, columns), BF),
        pltpu.VMEM((nb, half, columns), BF),
        pltpu.VMEM((half, columns), BF),
        pltpu.VMEM((nb - 1, half, columns), BF),
        pltpu.VMEM((nz - 1, rows, columns // nz), BF),
    ]


def key_parts(span, block):
    low = max(0, (block - 1) * ROWS)
    high = min(span, (block + 2) * ROWS)
    if low <= ROWS:
        return [(0, high)]
    return [(0, ROWS), (low, high)]


def head_masks():
    lane = lax.broadcasted_iota(jnp.int32, (1, LANES), 1)
    return (lane < HD, lane >= HD)


def only(mask, block):
    return jnp.where(mask, block, jnp.zeros_like(block))


def make_bias(marks_ref, bias):
    span = bias.shape[0]
    for i in range(0, span, ROWS):
        part = slice(i, i + ROWS)
        distance = lax.broadcasted_iota(jnp.int32, (ROWS, span), 0) + i - lax.broadcasted_iota(jnp.int32, (ROWS, span), 1)
        near = jnp.where(jnp.abs(distance) <= W // 2, 0.0, NEGATIVE)
        near = jnp.where(marks_ref[part, 1:2] > 0.5, 0.0, near)
        bias[part, :] = jnp.where(marks_ref[part, 0:1] > 0.5, near, NEGATIVE)


def attend_local(refs, bias_ref, a_ref, lse_ref, tick):
    k_ref, v_ref, q_ref = refs
    span = q_ref.shape[0]
    masks = head_masks()
    query = q_ref[...] * jnp.asarray(HD ** (-0.5), BF)
    values_flip = v_ref[...].T
    for block in range(span // ROWS):
        tick(block)
        rows = slice(block * ROWS, (block + 1) * ROWS)
        parts = key_parts(span, block)
        flips = []
        for h in range(2):
            head_query = only(masks[h], query[rows])
            scored = [
                product_back(k_ref[lo:hi, :], head_query) + bias_ref[lo:hi, rows] for lo, hi in parts
            ]
            top = jnp.max(scored[0], axis=0, keepdims=True)
            for s in scored[1:]:
                top = jnp.maximum(top, jnp.max(s, axis=0, keepdims=True))
            weights = [jnp.exp(s - top) for s in scored]
            total = sum(jnp.sum(w, axis=0, keepdims=True) for w in weights)
            lse_ref[0, h : h + 1, rows] = top + jnp.log(total)
            mixed = sum(
                product(values_flip[h * HD : (h + 1) * HD, lo:hi], w.astype(BF))
                for (lo, hi), w in zip(parts, weights)
            )
            flips.append(mixed * (1.0 / total))
        a_ref[rows, :] = jnp.concatenate(flips, axis=0).T.astype(BF)


def attend_global(refs, qg_ref, marks_ref, place_ref, a_ref, lse_global_ref):
    kg_ref, vg_ref = refs
    masks = head_masks()
    query = qg_ref[...] * jnp.asarray(HD ** (-0.5), BF)
    stacked = jnp.concatenate([only(m, query) for m in masks], axis=0)
    scores = product_back(kg_ref[...], stacked) + jnp.where(marks_ref[:, 0:1] > 0.5, 0.0, NEGATIVE)
    top = jnp.max(scores, axis=0, keepdims=True)
    probs = jnp.exp(scores - top)
    total = jnp.sum(probs, axis=0, keepdims=True)
    lse_global_ref[...] = jnp.broadcast_to(top + jnp.log(total), (8, LANES))
    probs = (probs * (1.0 / total)).astype(BF)
    mixed = product_left(probs, vg_ref[...])
    global_out = jnp.where(masks[0], mixed[:NG], mixed[NG:]).astype(BF)
    global_rows = product(place_ref[...], global_out)
    is_global = marks_ref[:ROWS, 1:2] > 0.5
    a_ref[:ROWS, :] = jnp.where(is_global, global_rows, a_ref[:ROWS, :].astype(F32)).astype(BF)


def attention_backward(refs, qg_ref, bias_ref, marks_ref, place_ref, a_ref, da_ref, lse_ref, lse_global_ref,
                       back_refs, dqg_ref, sums_ref, dk_sum, dv_sum, tick):
    k_ref, v_ref, q_ref, kg_ref, vg_ref = refs
    dk_ref, dv_ref, dq_ref, dkg_ref, dvg_ref = back_refs
    span = q_ref.shape[0]
    masks = head_masks()
    scale = HD ** (-0.5)
    query = q_ref[...] * jnp.asarray(scale, BF)
    keys_flip = k_ref[...].T
    query_global = qg_ref[...] * jnp.asarray(scale, BF)
    stacked = jnp.concatenate([only(m, query_global) for m in masks], axis=0)
    adjoint_global = product_left(place_ref[...], da_ref[:ROWS, :]).astype(BF)
    adjoint_stacked = jnp.concatenate([only(m, adjoint_global) for m in masks], axis=0)
    scores = product_back(kg_ref[...], stacked) + jnp.where(marks_ref[:, 0:1] > 0.5, 0.0, NEGATIVE)
    probs = jnp.exp(scores - lse_global_ref[0, 0:1, :])
    prob_adjoint = product_back(vg_ref[...], adjoint_stacked)
    center = jnp.sum(probs * prob_adjoint, axis=0, keepdims=True)
    score_adjoint = (probs * (prob_adjoint - center)).astype(BF)
    mixed = product_left(score_adjoint, kg_ref[...]) * scale
    dqg_ref[...] = jnp.where(masks[0], mixed[:NG], mixed[NG:]).astype(BF)
    dkg_ref[...] = product(score_adjoint, stacked).astype(BF)
    dvg_ref[...] = product(probs.astype(BF), adjoint_stacked).astype(BF)
    first = jnp.where(marks_ref[:ROWS, 1:2] > 0.5, 0.0, da_ref[:ROWS, :].astype(F32)).astype(BF)
    adjoint = jnp.concatenate([first, da_ref[ROWS:, :]], axis=0)
    inner = adjoint.astype(F32) * a_ref[...].astype(F32)
    picker = (lax.broadcasted_iota(jnp.int32, (8, LANES), 0) == lax.div(lax.broadcasted_iota(jnp.int32, (8, LANES), 1), HD)).astype(F32)
    centers = lax.dot_general(
        picker, inner, (((1,), (1,)), ((), ())), preferred_element_type=F32, precision=lax.Precision.HIGHEST
    )
    dk_sum[...] = jnp.zeros_like(dk_sum)
    dv_sum[...] = jnp.zeros_like(dv_sum)
    for block in range(span // ROWS):
        tick(block)
        rows = slice(block * ROWS, (block + 1) * ROWS)
        parts = key_parts(span, block)
        flips = []
        for h in range(2):
            head_query = only(masks[h], query[rows])
            head_adjoint = only(masks[h], adjoint[rows])
            log_sum = lse_ref[0, h : h + 1, rows]
            center = centers[h : h + 1, rows]
            mixed = None
            for lo, hi in parts:
                s = product_back(k_ref[lo:hi, :], head_query) + bias_ref[lo:hi, rows]
                weights = jnp.exp(s - log_sum)
                prob_adjoint = product_back(v_ref[lo:hi, :], head_adjoint)
                score_adjoint = (weights * (prob_adjoint - center)).astype(BF)
                dv_sum[lo:hi, :] += product(weights.astype(BF), head_adjoint)
                dk_sum[lo:hi, :] += product(score_adjoint, head_query)
                part = product(keys_flip[h * HD : (h + 1) * HD, lo:hi], score_adjoint)
                mixed = part if mixed is None else mixed + part
            flips.append(mixed)
        dq_ref[rows, :] = (jnp.concatenate(flips, axis=0).T * scale).astype(BF)
    dk_ref[...] = dk_sum[...].astype(BF)
    dv_ref[...] = dv_sum[...].astype(BF)
    sums = [jnp.sum(r[...].astype(F32), axis=0, keepdims=True) for r in (dq_ref, dv_ref, dqg_ref, dvg_ref)]
    sums_ref[...] = jnp.concatenate(sums + [jnp.zeros((4, LANES), F32)], axis=0)


def gelu_and_slope(u):
    e = jnp.exp2(u * (u * (-0.5 * 1.4426950408889634)))
    t = 1.0 / (1.0 + (0.3275911 * 0.7071067811865476) * jnp.abs(u))
    tail = 0.5 * -1.453152027 + t * (0.5 * 1.061405429)
    tail = 0.5 * -0.284496736 + t * (0.5 * 1.421413741 + t * tail)
    tail = t * (0.5 * 0.254829592 + t * tail) * e
    phi = jnp.where(u >= 0.0, 1.0 - tail, tail)
    return u * phi, phi + u * e * 0.3989422804014327


def normalize(mixture):
    centered = mixture - jnp.mean(mixture, axis=-1, keepdims=True)
    spread = lax.rsqrt(jnp.mean(centered * centered, axis=-1, keepdims=True) + EPS_NORM)
    return centered * spread, spread


def normalize_back(adjoint, normal, spread, gain):
    scaled = adjoint * gain
    mean = jnp.mean(scaled, axis=-1, keepdims=True)
    along = jnp.mean(scaled * normal, axis=-1, keepdims=True)
    return spread * (scaled - mean - normal * along)


def kernel_params(collective=None, **more):
    if collective is not None:
        more.update(collective_id=collective, has_side_effects=True)
    return pltpu.CompilerParams(vmem_limit_bytes=61 * MIB, **more)


def dma(count):
    return pltpu.SemaphoreType.DMA((count,))


def still(*shape):
    return pl.BlockSpec(shape, lambda s: (0,) * len(shape), pipeline_mode=pl.Buffered(1))


def full_shape(nb, block, columns, *lead):
    return lead + (2, nb, 2, block, columns)


def everyone(spot):
    devices = spot.groups * spot.nz
    me = spot.g * spot.nz + spot.z
    ids = [lax.rem(me + i, devices) for i in range(1, devices)]
    return [(lax.div(i, spot.nz), lax.rem(i, spot.nz)) for i in ids]


def project_and_attend(mesh, low_in, low_rest, low_vectors, sequence, place, marks, parts):
    groups, depth = mesh.shape["grp"], mesh.shape["dp"]
    nb = groups // 4
    count, block, width = low_in.shape
    rest = low_rest.shape[0]
    span, columns = sequence.shape
    devices = groups * depth
    few = place.shape[1]
    pairs = H // 2
    total = (count + rest) * gather_copies(nb, depth) + depth - 1 + devices - 1
    lag = 3
    local_count = 3
    attend = lag + local_count
    project = attend + pairs
    glob = project + count - local_count
    together = 2
    steps = glob + pairs // together

    def slot(s):
        return 4 * s if s < attend else 4 * attend + 6 * (s - attend)

    def kernel(in_ref, rest_ref, vec_ref, seq_ref, place_ref, marks_ref, part_ref,
               full_ref, out_ref, up_ref, vec_full_ref, proj_ref, few_ref, a_ref, lse_ref, lse_global_ref, swapped_ref,
               weight, vec, proj, bias, send, recv, local):
        spot = Spot(groups, depth)
        sems = Sems(send, recv)
        pairs_of = [(in_ref.at[t], full_ref.at[t]) for t in range(count)]
        pairs_of += [(rest_ref.at[0], out_ref)] + [(rest_ref.at[1 + q], up_ref.at[q]) for q in range(rest - 1)]
        pieces = [GatherPiece(spot, sems, local.at[t], src, out) for t, (src, out) in enumerate(pairs_of)]
        swap = Swap(spot, sems, local.at[count + rest], part_ref, swapped_ref)
        own = pl.ds(pl.multiple_of(spot.z * width, LANES), width)
        mine = vec_full_ref.at[:, own]
        vec_local = pltpu.make_async_copy(vec_ref, mine, local.at[count + rest + 1])
        vec_sends = [sems.copy(vec_ref, mine, spot.at(z=spot.z_off(i))) for i in range(1, depth)]
        keep = [
            pltpu.make_async_copy(proj.at[t], proj_ref.at[t], local.at[count + rest + 2 + t]) for t in range(count - 1)
        ]
        step = pl.program_id(0)
        ticks = Ticks(4)
        times = slot_times(slot, count + rest)
        for t in range(local_count, count + rest):
            times[t] = [slot(t - 2) + 1, slot(t), slot(t + 2) + 1, slot(t + 4) + 2, slot(t + 5) + 3]
        ticks.add_all(timeline(pieces, times))
        for j in range(8):
            ticks.add(4 * (attend + 2 * j if j < 4 else project + j - 4) + 2, lambda j=j: swap.start(j, 8))

        @pl.when(step == 0)
        def _():
            greet(everyone(spot))
            vec_local.start()
            start_all(vec_sends)

        for c in range(4):
            ticks.here(c, 0, attend - 1)

        @pl.when(step == 0)
        def _():
            make_bias(marks_ref, bias)

        @pl.when(step == lag)
        def _():
            vec_local.wait()
            recv_all(vec_sends)
            send_done(vec_sends)
            pltpu.sync_copy(vec_full_ref, vec)

        def offset(row):
            index = lax.broadcasted_iota(jnp.int32, vec.shape, 0)
            return jnp.sum(jnp.where(index == row, vec[...].astype(F32), 0.0), axis=0, keepdims=True)

        for c in range(4):
            ticks.here(c, project, steps - 1)

        def project_one(t):
            pltpu.sync_copy(full_ref.at[t], weight)
            added = offset(jnp.where(t == 1, 1, jnp.where(t == 2, 0, jnp.where(t == 4, 4, 15))))

            def body(rows):
                matrix = weight[...].reshape(groups * block, columns)
                proj[t, rows, :] = (product(seq_ref[rows, :], matrix) + added).astype(BF)

            in_chunks(span, body)

        first_part = jnp.logical_and(step >= lag, step < attend)
        second_part = jnp.logical_and(step >= project, step < glob - 1)
        pl.when(jnp.logical_or(first_part, second_part))(
            lambda: project_one(jnp.where(step < attend, step - lag, step - project + local_count))
        )
        for t in range(count - 1):
            pl.when(step == (lag + t if t < local_count else project + t - local_count))(keep[t].start)

        @pl.when(step == glob - 1)
        def _():
            pltpu.sync_copy(full_ref.at[count - 1], weight)
            matrix = weight[...].reshape(groups * block, columns)
            rows = product_left(place_ref[...], seq_ref[:ROWS, :]).astype(BF)
            few_ref[...] = (product(rows, matrix) + offset(3)).astype(BF)

        @during(attend, project - 1)
        def _():
            lanes = pl.ds(pl.multiple_of((step - attend) * LANES, LANES), LANES)
            attend_local(
                [proj.at[i, :, lanes] for i in range(local_count)], bias, a_ref.at[:, lanes], lse_ref,
                lambda c: ticks.here(c, attend, project - 1),
            )

        @pl.when(step >= glob)
        def _():
            def one(i, carry):
                pair = (step - glob) * together + i
                lanes = pl.ds(pl.multiple_of(pair * LANES, LANES), LANES)
                attend_global(
                    [proj.at[i, :, lanes] for i in range(local_count, count - 1)], few_ref.at[:, lanes], marks_ref, place_ref,
                    a_ref.at[:, lanes], lse_global_ref.at[pair],
                )
                return carry

            lax.fori_loop(0, together, one, 0)

        @pl.when(step == steps - 1)
        def _():
            for copy in keep:
                copy.wait()
            swap.finish()

    at = lambda s: jnp.clip(s - attend, 0, pairs - 1)
    results = pl.pallas_call(
        kernel,
        grid=(steps,),
        in_specs=[ANYSPEC] * 3 + [still(span, columns), still(*place.shape), still(*marks.shape), ANYSPEC],
        out_specs=[ANYSPEC] * 5
        + [
            pl.BlockSpec((few, columns), lambda s: (0, 0)),
            pl.BlockSpec((span, columns), lambda s: (0, 0)),
            pl.BlockSpec((1, 8, span), lambda s: (at(s), 0, 0)),
            pl.BlockSpec((pairs, 8, LANES), lambda s: (0, 0, 0)),
            ANYSPEC,
        ],
        out_shape=[
            jax.ShapeDtypeStruct(full_shape(nb, block, columns, count), BF),
            jax.ShapeDtypeStruct(full_shape(nb, block, columns), BF),
            jax.ShapeDtypeStruct(full_shape(nb, block, columns, rest - 1), BF),
            jax.ShapeDtypeStruct((low_vectors.shape[0], columns), BF),
            jax.ShapeDtypeStruct((count - 1, span, columns), BF),
            jax.ShapeDtypeStruct((few, columns), BF),
            jax.ShapeDtypeStruct((span, columns), BF),
            jax.ShapeDtypeStruct((pairs, 8, span), F32),
            jax.ShapeDtypeStruct((pairs, 8, LANES), F32),
            jax.ShapeDtypeStruct(parts.shape, BF),
        ],
        scratch_shapes=[
            pltpu.VMEM(full_shape(nb, block, columns), BF),
            pltpu.VMEM((low_vectors.shape[0], columns), BF),
            pltpu.VMEM((count - 1, span, columns), BF),
            pltpu.VMEM((span, span), F32),
            dma(total),
            dma(total),
            dma(count + rest + 2 + count - 1),
        ],
        compiler_params=kernel_params(0),
        name="project_and_attend",
    )(low_in, low_rest, low_vectors, sequence, place, marks, parts)
    square = (groups * block, columns)
    full_in, full_out, full_up = results[:3]
    return (full_in.reshape((count,) + square), full_out.reshape(square), full_up.reshape((rest - 1,) + square)) + tuple(
        results[3:]
    )


def feed_forward(mesh, sequence, attended, full_out, full_up, shards, parts, vectors, hidden_bias, valid):
    groups, depth = mesh.shape["grp"], mesh.shape["dp"]
    nb = groups // 4
    span, columns = sequence.shape
    count, block, width = shards.shape
    devices = groups * depth
    total = count * gather_copies(nb, depth) + devices - 1
    steps = count + 3
    extra = FF // D

    def kernel(seq_ref, att_ref, wo_ref, up_ref, shard_ref, part_ref, vec_ref, hb_ref, valid_ref,
               full_ref, hid_ref, slope_ref, low_ref, normal_ref, spread_ref, layer_ref, feed_low_ref, sum_ref, sums_ref,
               first, low, normal, hidden, feed, weight, cot, send, recv, local):
        spot = Spot(groups, depth)
        sems = Sems(send, recv)
        pieces = [GatherPiece(spot, sems, local.at[t], shard_ref.at[t], full_ref.at[t]) for t in range(count)]
        swap = Swap(spot, sems, local.at[count], part_ref, cot)
        keep_low = pltpu.make_async_copy(low, low_ref, local.at[count + 1])
        keep_normal = pltpu.make_async_copy(normal, normal_ref, local.at[count + 2])
        keep_hidden = [
            pltpu.make_async_copy(hidden.at[q], hid_ref.at[q], local.at[count + 3 + q]) for q in range(count)
        ]
        keep_sum = pltpu.make_async_copy(feed, sum_ref, local.at[2 * count + 3])
        step = pl.program_id(0)

        @pl.when(step == 0)
        def _():
            greet(everyone(spot))

        ticks = Ticks(8)
        starts = [[0, 1, 2, 3], [8, 16, 24, 32], [10, 19, 28, 37], [18, 27, 36, 45], [25, 34, 44, 52]]
        ticks.add_all(timeline(pieces, [[starts[p][q] for p in range(5)] for q in range(count)]))
        for j, tick in enumerate((3, 5, 8, 9, 10, 11, 16, 17)):
            ticks.add(tick, lambda j=j: swap.start(j, 8))
        chunks = [slice(i, i + ROWS) for i in range(0, span, ROWS)]

        def work(first, last, offset, body):
            @during(first, last)
            def _():
                for c, rows in enumerate(chunks):
                    ticks.here(offset + c, first, last)
                    body(rows)

        def idle(first, last, offset):
            for c in range(len(chunks)):
                ticks.here(offset + c, first, last)

        def norm(rows):
            mixture = seq_ref[rows, :].astype(F32) + product(att_ref[rows, :], wo_ref[...]) + vec_ref[2:3, :]
            centered, spread = normalize(mixture)
            out = centered * vec_ref[6 + extra : 7 + extra, :] + vec_ref[7 + extra : 8 + extra, :]
            first[rows, :] = out
            low[rows, :] = out.astype(BF)
            feed[rows, :] = jnp.broadcast_to(vec_ref[5 + extra : 6 + extra, :], (ROWS, columns))
            normal[rows, :] = centered.astype(BF)
            spread_ref[rows, :] = jnp.broadcast_to(spread, (ROWS, LANES))

        def up(rows):
            q = step - 1
            u = product(low[rows, :], up_ref[0]) + hb_ref[pl.ds(q, 1), :]
            act, slope = gelu_and_slope(u)
            hidden[q, rows, :] = act.astype(BF)
            slope_ref[0, rows, :] = slope.astype(BF)

        def down(rows):
            part = product(hidden[step - 3, rows, :], weight[...].reshape(groups * block, columns))
            feed[rows, :] += part

        work(0, 0, 0, norm)

        @pl.when(step == 0)
        def _():
            keep_low.start()
            keep_normal.start()

        idle(0, 2, 4)
        work(1, count, 0, up)
        for q in range(count):
            pl.when(step == q + 1)(keep_hidden[q].start)
        idle(count + 1, steps - 1, 0)
        for q in range(count):

            @pl.when(step == q + 3)
            def _(q=q):
                ticks.here(4, q + 3, q + 3)
                pltpu.sync_copy(full_ref.at[q], weight)

        @during(3, steps - 1)
        def _():
            for c, rows in enumerate(chunks):
                if c:
                    ticks.here(4 + c, 3, steps - 1)
                down(rows)


        @pl.when(step == steps - 1)
        def _():
            swap.finish()
            sums_ref[...] = jnp.zeros_like(sums_ref)
            pieces_of = span // devices

            def body(rows):
                part = pl.ds(rows.start // pieces_of, ROWS // pieces_of)
                mask = valid_ref[rows, 0:1]
                cotangent = cot[part].reshape(ROWS, columns).astype(F32) * mask
                gain = vec_ref[8 + extra : 9 + extra, :]
                mixture = first[rows, :] + feed[rows, :]
                centered, spread = normalize(mixture)
                layer_ref[rows, :] = ((centered * gain + vec_ref[9 + extra : 10 + extra, :]) * mask).astype(BF)
                back = normalize_back(cotangent, centered, spread, gain)
                back_low = back.astype(BF)
                feed[rows, :] = back
                feed_low_ref[rows, :] = back_low
                sums_ref[0:1, :] += jnp.sum(back_low.astype(F32), axis=0, keepdims=True)
                sums_ref[1:2, :] += jnp.sum(cotangent * centered, axis=0, keepdims=True)
                sums_ref[2:3, :] += jnp.sum(cotangent, axis=0, keepdims=True)

            in_chunks(span, body)
            keep_sum.start()
            keep_low.wait()
            keep_normal.wait()
            for copy in keep_hidden:
                copy.wait()
            keep_sum.wait()

    matrix = lambda kind: jax.ShapeDtypeStruct((span, columns), kind)
    stack = jax.ShapeDtypeStruct((count, span, columns), BF)
    by_q = pl.BlockSpec((1, span, columns), lambda s: (jnp.clip(s - 1, 0, count - 1), 0, 0))
    results = pl.pallas_call(
        kernel,
        grid=(steps,),
        in_specs=[
            still(span, columns), still(span, columns), still(*full_out.shape), by_q, ANYSPEC, ANYSPEC,
            still(*vectors.shape), still(*hidden_bias.shape), still(*valid.shape),
        ],
        out_specs=[ANYSPEC, ANYSPEC, by_q, ANYSPEC, ANYSPEC]
        + [pl.BlockSpec((span, LANES), lambda s: (0, 0))]
        + [pl.BlockSpec((span, columns), lambda s: (0, 0))] * 2
        + [ANYSPEC, pl.BlockSpec((8, columns), lambda s: (0, 0))],
        out_shape=[
            jax.ShapeDtypeStruct(full_shape(nb, block, columns, count), BF), stack, stack, matrix(BF), matrix(BF),
            jax.ShapeDtypeStruct((span, LANES), F32), matrix(BF), matrix(BF), matrix(F32),
            jax.ShapeDtypeStruct((8, columns), F32),
        ],
        scratch_shapes=[
            pltpu.VMEM((span, columns), F32),
            pltpu.VMEM((span, columns), BF),
            pltpu.VMEM((span, columns), BF),
            pltpu.VMEM((count, span, columns), BF),
            pltpu.VMEM((span, columns), F32),
            pltpu.VMEM(full_shape(nb, block, columns), BF),
            pltpu.VMEM(parts.shape, BF),
            dma(total),
            dma(total),
            dma(2 * count + 4),
        ],
        compiler_params=kernel_params(1),
        name="feed_forward",
    )(sequence, attended, full_out, full_up, shards, parts, vectors, hidden_bias, valid)
    return (results[0].reshape(count, groups * block, columns),) + tuple(results[1:])


def feed_backward(mesh, feed_low, low, hidden, slope, full_up, full_down, sum_adjoint, attended, full_out, normal, spread,
                  gain, parts):
    groups, depth = mesh.shape["grp"], mesh.shape["dp"]
    nb = groups // 4
    span, columns = feed_low.shape
    count = hidden.shape[0]
    block, width = columns // groups, columns // depth
    devices = groups * depth
    half = columns // 2
    total = count * reduce_copies(nb, depth) + devices - 1
    work = 3 * count
    steps = work + 2
    boxes = [reduce_boxes(nb, depth, block, columns) for _ in range(count)]
    per = len(boxes[0])

    def kernel(feed_ref, low_ref, hid_ref, slope_ref, up_ref, down_ref, sum_ref, att_ref, wo_ref, normal_ref, spread_ref,
               gain_ref, part_ref,
               change_ref, hb_ref, mix_ref, own_ref, swapped_ref, out_change_ref, att_back_ref, sums_ref,
               back_low, norm, branch, send, recv, local, *box_refs):
        spot = Spot(groups, depth)
        sems = Sems(send, recv)
        tiles = [box_refs[q * per] for q in range(count)]

        def finish(q):
            def store(value):
                own_ref[q] = value

            return store

        pieces = [
            ReducePiece(spot, sems, None, None, width, box_refs[q * per : (q + 1) * per], finish(q)) for q in range(count)
        ]
        swap = Swap(spot, sems, local.at[0], part_ref, swapped_ref)
        keep = pltpu.make_async_copy(norm, mix_ref, local.at[1])
        fetch = pltpu.make_async_copy(sum_ref, norm, local.at[2])
        step = pl.program_id(0)
        ticks = Ticks(4)
        starts = [[3, 7, 11, 15], [7, 19, 27, 35], [17, 25, 33, 41], [22, 30, 38, 46], [31, 39, 47, 53]]
        ticks.add_all(timeline(pieces, [[starts[p][q] for p in range(5)] for q in range(count)]))
        for j in range(8):
            ticks.add(4 * (j + 2), lambda j=j: swap.start(j, 8))
        chunks = [slice(i, i + ROWS) for i in range(0, span, ROWS)]

        def work_on(first, last, body):
            for c, rows in enumerate(chunks):
                if c == len(chunks) // 2:
                    ticks.here(1, first, last)
                body(rows)
            ticks.here(2, first, last)

        @pl.when(step == 0)
        def _():
            greet(everyone(spot))
            fetch.start()

        ticks.here(0, 0, steps - 1)

        for q in range(count):

            @pl.when(step == q)
            def _(q=q):
                value = product_left(hid_ref[0], feed_ref[...]).astype(BF)
                tiles[q][...] = value.reshape(full_shape(nb, block, columns))

        pl.when(step == count)(fetch.wait)

        for c in (1, 2):
            ticks.here(c, 0, count - 1)

        @during(count, work - 1)
        def _():
            hb_ref[...] = jnp.zeros_like(hb_ref)

            def body(rows):
                value = product_back(feed_ref[rows, :], down_ref[0]) * slope_ref[0, rows, :].astype(F32)
                value = value.astype(BF)
                back_low[rows, :] = value
                hb_ref[0] += jnp.broadcast_to(jnp.sum(value.astype(F32), axis=0, keepdims=True), (8, half))
                norm[rows, :] += product_back(value, up_ref[0])

            work_on(count, work - 1, body)
            change_ref[0] = product_left(low_ref[...], back_low[...]).astype(BF)

        @pl.when(step == work)
        def _():
            sums_ref[...] = jnp.zeros_like(sums_ref)

            def body(rows):
                adjoint = norm[rows, :]
                centered = normal_ref[rows, :].astype(F32)
                back = normalize_back(adjoint, centered, spread_ref[rows, 0:1], gain_ref[0:1, :])
                back_branch = back.astype(BF)
                norm[rows, :] = back
                branch[rows, :] = back_branch
                sums_ref[0:1, :] += jnp.sum(back_branch.astype(F32), axis=0, keepdims=True)
                sums_ref[1:2, :] += jnp.sum(adjoint * centered, axis=0, keepdims=True)
                sums_ref[2:3, :] += jnp.sum(adjoint, axis=0, keepdims=True)
                att_back_ref[rows, :] = product_back(back_branch, wo_ref[...]).astype(BF)

            work_on(work, work, body)
            keep.start()
            out_change_ref[...] = product_left(att_ref[...], branch[...]).astype(BF)

        ticks.here(3, 0, work)
        for c in range(1, 4):
            ticks.here(c, work + 1, steps - 1)

        @pl.when(step == steps - 1)
        def _():
            keep.wait()
            swap.finish()

    at = lambda s: jnp.clip(s - count, 0, 2 * count - 1)
    by_half = pl.BlockSpec((1, span, half), lambda s: (lax.div(at(s), 2), 0, lax.rem(at(s), 2)))
    whole = lambda *dims: pl.BlockSpec(dims, lambda s: (0,) * len(dims))
    return pl.pallas_call(
        kernel,
        grid=(steps,),
        in_specs=[
            still(span, columns), still(span, columns),
            pl.BlockSpec((1, span, columns), lambda s: (jnp.minimum(s, count - 1), 0, 0)),
            by_half, by_half,
            pl.BlockSpec((1, half, columns), lambda s: (lax.div(at(s), 2), lax.rem(at(s), 2), 0)),
            ANYSPEC, still(span, columns), still(columns, columns), still(span, columns), still(span, LANES),
            still(8, columns), ANYSPEC,
        ],
        out_specs=[
            by_half,
            pl.BlockSpec((1, 8, half), lambda s: (lax.div(at(s), 2), 0, lax.rem(at(s), 2))),
            ANYSPEC, whole(count, block, width), ANYSPEC, whole(columns, columns), whole(span, columns), whole(8, columns),
        ],
        out_shape=[
            jax.ShapeDtypeStruct((count, columns, columns), BF),
            jax.ShapeDtypeStruct((count, 8, columns), F32),
            jax.ShapeDtypeStruct((span, columns), F32),
            jax.ShapeDtypeStruct((count, block, width), F32),
            jax.ShapeDtypeStruct(parts.shape, BF),
            jax.ShapeDtypeStruct((columns, columns), BF),
            jax.ShapeDtypeStruct((span, columns), BF),
            jax.ShapeDtypeStruct((8, columns), F32),
        ],
        scratch_shapes=[
            pltpu.VMEM((span, half), BF),
            pltpu.VMEM((span, columns), F32),
            pltpu.VMEM((span, columns), BF),
            dma(total),
            dma(total),
            dma(3),
        ]
        + [box for some in boxes for box in some],
        compiler_params=kernel_params(2),
        name="feed_backward",
    )(feed_low, low, hidden, slope, full_up, full_down, sum_adjoint, attended, full_out, normal, spread, gain, parts)


def attend_back_and_reduce(mesh, projected, query_global, marks, place, attended, attended_adjoint, log_sums, log_sums_global,
                           changes, parts, full_in, sequence, mixture_adjoint, hidden_sums, feed_sums, norm_sums, order):
    groups, depth = mesh.shape["grp"], mesh.shape["dp"]
    nb = groups // 4
    span, columns = sequence.shape
    pairs = H // 2
    count = full_in.shape[0]
    few = query_global.shape[0]
    block, width = columns // groups, columns // depth
    devices = groups * depth
    views = [c.reshape((-1,) + full_shape(nb, block, columns)) for c in changes]
    where = [(i, t) for i, v in enumerate(views) for t in range(v.shape[0])]
    early = len(where)
    given = len(views)
    vec_rows = 16
    extra = hidden_sums.shape[0]
    total = (early + count) * reduce_copies(nb, depth) + devices - 1 + depth - 1 + groups - 1
    late_starts = [4 * (pairs + t) + 3 for t in range(count)]
    late_times = [[m, m + 3, m + 9, m + 12, m + 16] for m in late_starts]
    steps = late_times[-1][-1] // 4 + 1
    boxes = [reduce_boxes(nb, depth, block, columns) for _ in range(max(early + 1, count))]
    per = len(boxes[0])

    def kernel(*refs):
        stack_ref, few_ref, marks_ref, place_ref, a_ref, da_ref, lse_ref, lse_global_ref = refs[:8]
        change_refs, refs = refs[8 : 8 + given], refs[8 + given :]
        part_ref, weight_ref, seq_ref, mix_ref, hidden_ref, feed_ref, norm_ref = refs[:7]
        own_refs, own_in_ref, vec_out, grad_ref, swapped_ref = refs[7 : 7 + given], *refs[7 + given : 11 + given]
        refs = refs[11 + given :]
        bias, back, dqg, sums, dk_sum, dv_sum, grad, vec, vec_z, vec_g, send, recv, local, free = refs[:14]
        box_refs = refs[14:]
        spot = Spot(groups, depth)
        sems = Sems(send, recv)

        def finish(ref, i):
            def store(value):
                ref[i] = value

            return store

        box = lambda i: box_refs[i * per : (i + 1) * per]
        pieces = [
            ReducePiece(spot, sems, local.at[i], change_refs[v].at[t], width, box(i), finish(own_refs[v], t))
            for i, (v, t) in enumerate(where)
        ]
        late_box = [early] + list(range(early)) + list(range(early + 1, count))
        late = [
            ReducePiece(spot, sems, None, None, width, box(late_box[t]), finish(own_in_ref, int(order[t]))) for t in range(count)
        ]
        tiles = [box_refs[late_box[t] * per] for t in range(count)]
        swap = Swap(spot, sems, local.at[early], part_ref, swapped_ref)
        fetch = pltpu.make_async_copy(mix_ref, grad, local.at[early + 1])
        keep = pltpu.make_async_copy(back.at[0], grad_ref, local.at[early + 2])
        part = lambda zz: pl.ds(pl.multiple_of(zz * width, LANES), width)
        first = [
            sems.copy(vec.at[:, part(spot.z_off(i))], vec_z.at[i - 1], spot.at(z=spot.z_off(i)))
            for i in range(1, depth)
        ]
        second = [
            sems.copy(vec_g.at[spot.g], vec_g.at[spot.g], (lax.rem(spot.g + i, groups), spot.z))
            for i in range(1, groups)
        ]
        step = pl.program_id(0)
        ticks = Ticks(4)
        ticks.add_all(
            timeline(pieces, [[max(0, 5 * t - 3), 5 * t + 2, 5 * t + 6, 5 * t + 9, 5 * t + 13] for t in range(early)])
        )
        for j, tick in enumerate((1, 5, 9, 13, 17, 29, 32, 35)):
            ticks.add(tick, lambda j=j: swap.start(j, 8))

        def freed():
            for target in spot.neighbours():
                pl.semaphore_signal(free, inc=1, device_id=target, device_id_type=MESH)

        ticks.add(5 * (early - 1) + 13, freed)
        ticks.add(late_starts[1], lambda: pl.semaphore_wait(free, len(spot.neighbours())))
        ticks.add_all(timeline(late, late_times))

        @pl.when(step == 0)
        def _():
            greet(everyone(spot))
            fetch.start()
            make_bias(marks_ref, bias)

        @pl.when(step < pairs)
        def _():
            lanes = pl.ds(pl.multiple_of(step * LANES, LANES), LANES)
            attention_backward(
                [stack_ref.at[i] for i in range(5)], few_ref, bias, marks_ref, place_ref,
                a_ref, da_ref, lse_ref, lse_global_ref,
                [back.at[i, :, lanes] for i in range(5)], dqg.at[:, lanes], sums.at[:, lanes], dk_sum, dv_sum,
                lambda c: ticks.here(c, 0, pairs - 1),
            )

        @pl.when(step == pairs)
        def _():
            fetch.wait()
            vec[...] = jnp.zeros_like(vec)
            vec[0:2, :] = sums[0:2, :]
            vec[2:3, :] = norm_ref[0:1, :]
            vec[3:5, :] = sums[2:4, :]
            vec[5 : 5 + extra, :] = hidden_ref[...]
            vec[5 + extra : 6 + extra, :] = feed_ref[0:1, :]
            vec[6 + extra : 8 + extra, :] = norm_ref[1:3, :]
            vec[8 + extra : 10 + extra, :] = feed_ref[1:3, :]
            start_all(first)

        ticks.here(0, pairs, steps - 1)
        ticks.here(1, pairs, steps - 1)

        for t in range(count - 1):

            @pl.when(step == pairs + t)
            def _(t=t):
                value = product_left(seq_ref[...], back[t]).astype(BF)
                tiles[t][...] = value.reshape(full_shape(nb, block, columns))

        @during(pairs, pairs + count - 2)
        def _():
            def body(rows):
                grad[rows, :] += product_back(back[step - pairs, rows, :], weight_ref[0])

            in_chunks(span, body)

        @pl.when(step == pairs + count - 1)
        def _():
            rows = product_left(place_ref[...], seq_ref[:ROWS, :]).astype(BF)
            value = product_left(rows, dqg[...]).astype(BF)
            tiles[count - 1][...] = value.reshape(full_shape(nb, block, columns))
            extra = product_back(dqg[...], weight_ref[0])
            grad[:ROWS, :] += lax.dot_general(
                place_ref[...].astype(F32), extra, (((1,), (0,)), ((), ())),
                precision=lax.Precision.HIGHEST, preferred_element_type=F32,
            )
            back[0] = grad[...].astype(BF)
            keep.start()

        ticks.here(2, pairs, steps - 1)
        ticks.here(3, pairs, steps - 1)

        @pl.when(step == pairs + 1)
        def _():
            recv_all(first)
            mine = vec[:, part(spot.z)]
            for i in range(depth - 1):
                mine = mine + vec_z[i]
            vec_g[spot.g] = mine
            start_all(second)

        @pl.when(step == steps - 1)
        def _():
            recv_all(second)
            whole = vec_g[0]
            for i in range(1, groups):
                whole = whole + vec_g[i]
            vec_out[...] = whole
            send_done(first)
            send_done(second)
            keep.wait()
            swap.finish()

    at = lambda s: jnp.minimum(s, pairs - 1)
    whole = lambda *dims: pl.BlockSpec(dims, lambda s: (0,) * len(dims))
    column = lambda rows: pl.BlockSpec((rows, LANES), lambda s: (0, at(s)))
    return pl.pallas_call(
        kernel,
        grid=(steps,),
        in_specs=[
            pl.BlockSpec((5, span, LANES), lambda s: (0, 0, at(s))),
            column(few), still(*marks.shape), still(*place.shape), column(span), column(span),
            pl.BlockSpec((1, 8, span), lambda s: (at(s), 0, 0)),
            pl.BlockSpec((1, 8, LANES), lambda s: (at(s), 0, 0)),
        ]
        + [ANYSPEC] * (given + 1)
        + [
            pl.BlockSpec((1, columns, columns), lambda s: (jnp.clip(s - pairs, 0, count - 1), 0, 0)),
            still(span, columns), ANYSPEC, still(*hidden_sums.shape), still(*feed_sums.shape), still(*norm_sums.shape),
        ],
        out_specs=[whole(v.shape[0], block, width) for v in views]
        + [whole(count, block, width), whole(vec_rows, width), ANYSPEC, ANYSPEC],
        out_shape=[jax.ShapeDtypeStruct((v.shape[0], block, width), F32) for v in views]
        + [
            jax.ShapeDtypeStruct((count, block, width), F32),
            jax.ShapeDtypeStruct((vec_rows, width), F32),
            jax.ShapeDtypeStruct((span, columns), BF),
            jax.ShapeDtypeStruct(parts.shape, BF),
        ],
        scratch_shapes=[
            pltpu.VMEM((span, span), F32),
            pltpu.VMEM((5, span, columns), BF),
            pltpu.VMEM((few, columns), BF),
            pltpu.VMEM((8, columns), F32),
            pltpu.VMEM((span, LANES), F32),
            pltpu.VMEM((span, LANES), F32),
            pltpu.VMEM((span, columns), F32),
            pltpu.VMEM((vec_rows, columns), F32),
            pltpu.VMEM((depth - 1, vec_rows, width), F32),
            pltpu.VMEM((groups, vec_rows, width), F32),
            dma(total),
            dma(total),
            dma(early + 3),
            pltpu.SemaphoreType.REGULAR,
        ]
        + [box for some in boxes for box in some],
        compiler_params=kernel_params(3),
        name="attend_back_and_reduce",
    )(projected, query_global, marks, place, attended, attended_adjoint, log_sums, log_sums_global, *views, parts, full_in,
      sequence, mixture_adjoint, hidden_sums, feed_sums, norm_sums)


def up_parts(matrix, ratio, parts):
    rows, columns = matrix.shape
    r = columns // (ratio * parts)
    return matrix.reshape(rows, ratio, parts, r).transpose(2, 0, 1, 3).reshape(parts, rows, ratio * r)


def up_whole(stack, ratio):
    parts, rows, columns = stack.shape
    r = columns // ratio
    return stack.reshape(parts, rows, ratio, r).transpose(1, 2, 0, 3).reshape(rows, parts * columns)


def per_device(mesh, tokens, out_cotangent, lengths, places, deal, in_weights, out_weight, up_weight, down_weight, vectors,
               first_in, first_out, first_up, first_down, first_vectors,
               second_in, second_out, second_up, second_down, second_vectors):
    groups, depth = mesh.shape["grp"], mesh.shape["dp"]
    ratio = groups // depth
    devices = groups * depth
    span = tokens.shape[1]
    quarters = FF // D
    me = lax.axis_index(("grp", "dp"))
    ids = jnp.arange(devices, dtype=jnp.int32)
    inverse = jnp.sum(jnp.where(deal[None, :] == ids[:, None], ids[None, :], 0), axis=1)
    length = lengths[me]
    spots = places[me]
    sequence = tokens[0]
    order = np.array([1, 2, 0, 4, 5, 3])

    low_in = jnp.stack([in_weights[i] for i in order]).astype(BF)
    low_rest = jnp.concatenate([out_weight.astype(BF)[None], up_parts(up_weight.astype(BF), ratio, quarters)])
    low_down = down_weight.astype(BF).reshape(quarters, -1, down_weight.shape[1])
    nv = vectors.shape[0]
    low_vectors = jnp.pad(vectors, ((0, 16 - nv), (0, 0))).astype(BF)

    positions = jnp.arange(span, dtype=jnp.int32)
    is_global = jnp.any(positions[:, None] == spots[None, :], axis=1)
    lane = jnp.arange(LANES)[None, :]
    marks = jnp.where(lane == 0, (positions < length)[:, None], (lane == 1) & is_global[:, None]).astype(F32)
    place = (positions[:ROWS, None] == spots[None, :]).astype(BF)
    shape_parts = (devices, span // devices, D)

    (full_in, full_out, full_up, full_vectors, projected, query_global, attended, log_sums, log_sums_global,
     cotangent_parts) = project_and_attend(
        mesh, low_in, low_rest, low_vectors, sequence, place, marks, out_cotangent.reshape(shape_parts)
    )
    vector_rows = full_vectors.astype(F32)
    hidden_bias = vector_rows[5 : 5 + quarters].reshape(groups, quarters, -1).transpose(1, 0, 2).reshape(quarters, D)
    cotangent_parts = cotangent_parts.at[deal].get(mode="promise_in_bounds")
    full_down, hidden, slope, first_low, normal_one, spread_one, layer_out, feed_low, sum_adjoint, feed_sums = feed_forward(
        mesh, sequence, attended, full_out, full_up, low_down, cotangent_parts, vector_rows, hidden_bias, marks
    )
    gain_one = jnp.broadcast_to(vector_rows[6 + quarters][None], (8, D))
    up_change, hidden_sums, mixture_adjoint, part_down, layer_parts, out_change, attended_adjoint, norm_sums = feed_backward(
        mesh, feed_low, first_low, hidden, slope, full_up, full_down, sum_adjoint, attended, full_out, normal_one, spread_one,
        gain_one, layer_out.reshape(shape_parts)
    )
    layer_parts = layer_parts.at[inverse].get(mode="promise_in_bounds")
    hidden_bias_change = hidden_sums[:, 0].reshape(quarters, groups, -1).transpose(1, 0, 2).reshape(quarters, D)
    part_up, part_out, part_in, part_vectors, token_gradient, layer_mine = attend_back_and_reduce(
        mesh, projected, query_global, marks, place, attended, attended_adjoint, log_sums, log_sums_global,
        (up_change, out_change), layer_parts, full_in, sequence, mixture_adjoint, hidden_bias_change, feed_sums, norm_sums,
        order
    )

    step_count = jnp.float32(STEP)
    fix_first = 1.0 - jnp.power(jnp.float32(BETA_FIRST), step_count)
    fix_second = 1.0 - jnp.power(jnp.float32(BETA_SECOND), step_count)

    def adam(weight, gradient, moment, square, decay):
        return adam_update(weight, gradient, moment, square, decay, fix_first, fix_second)

    part_up = up_whole(part_up, ratio)
    part_out = part_out[0]
    part_down = part_down.reshape(down_weight.shape)
    update_in, moment_in, square_in = adam(in_weights, part_in, first_in, second_in, WEIGHT_DECAY)
    update_out, moment_out, square_out = adam(out_weight, part_out, first_out, second_out, WEIGHT_DECAY)
    update_up, moment_up, square_up = adam(up_weight, part_up, first_up, second_up, WEIGHT_DECAY)
    update_down, moment_down, square_down = adam(down_weight, part_down, first_down, second_down, WEIGHT_DECAY)
    update_vectors, moment_vectors, square_vectors = adam(vectors, part_vectors[:nv], first_vectors, second_vectors, 0.0)
    return (
        layer_mine.reshape(tokens.shape), token_gradient[None],
        update_in, update_out, update_up, update_down, update_vectors,
        moment_in, moment_out, moment_up, moment_down, moment_vectors,
        square_in, square_out, square_up, square_down, square_vectors,
    )


def solution(mesh):
    sequences = P(("grp", "dp"), None, None)
    stack, matrix, rows = P(None, "grp", "dp"), P("grp", "dp"), P(None, "dp")
    packed = (stack, matrix, matrix, matrix, rows)
    return jax.shard_map(
        lambda *arrays: per_device(mesh, *arrays),
        mesh=mesh,
        in_specs=(sequences, sequences, P(), P(), P()) + packed * 3,
        out_specs=(sequences, sequences) + packed * 3,
        check_vma=False,
    )
```

```python
import jax
import jax.numpy as jnp
import numpy as np
from jax import lax
from jax.experimental import pallas as pl
from jax.experimental.pallas import tpu as pltpu
from jax.sharding import PartitionSpec as P

D = 1024
H = 16
HD = 64
FF = 4096
W = 512
NG = 64
STEP = 10

EPS_NORM = 1e-05
WEIGHT_DECAY = 0.1
BETA_FIRST = 0.5
BETA_SECOND = 0.999
EPS_ADAM = 1e-08
NEGATIVE = -1e30

MESH = pl.DeviceIdType.MESH
MIB = 1 << 20
BF = jnp.bfloat16
F32 = jnp.float32
LANES = 128
ROWS = 256
ANYSPEC = pl.BlockSpec(memory_space=pl.ANY)
VMEMSPEC = pl.BlockSpec(memory_space=pltpu.VMEM)


def product(left_side, right_side):
    return jnp.dot(left_side, right_side, preferred_element_type=F32)


def product_back(left_side, right_side):
    return lax.dot_general(
        left_side, right_side, (((1,), (1,)), ((), ())), preferred_element_type=F32
    )


def product_left(left_side, right_side):
    return lax.dot_general(
        left_side, right_side, (((0,), (0,)), ((), ())), preferred_element_type=F32
    )


def column_sums(matrix):
    return jnp.sum(matrix.astype(F32), axis=0)


def adam_update(weight, gradient, moment, square, decay_rate, fix_first, fix_second):
    moment_new = BETA_FIRST * moment + (1.0 - BETA_FIRST) * gradient
    square_new = BETA_SECOND * square + (1.0 - BETA_SECOND) * gradient * gradient
    update = moment_new / fix_first / (jnp.sqrt(square_new / fix_second) + EPS_ADAM)
    return (update + decay_rate * weight, moment_new, square_new)


class Spot:
    def __init__(self, groups, depth):
        self.nb = groups // 4
        self.nz = depth
        self.groups = groups
        g = lax.axis_index("grp")
        self.g = g
        self.z = lax.axis_index("dp")
        self.c = lax.rem(g, 2)
        self.b = lax.rem(lax.div(g, 2), self.nb)
        self.a = lax.div(g, 2 * self.nb)

    def at(self, a=None, b=None, c=None, z=None):
        a = self.a if a is None else a
        b = self.b if b is None else b
        c = self.c if c is None else c
        z = self.z if z is None else z
        return ((a * self.nb + b) * 2 + c, z)

    def b_off(self, i):
        return lax.rem(self.b + i, self.nb)

    def z_off(self, i):
        return lax.rem(self.z + i, self.nz)

    def z_flip(self, bit):
        return self.z + bit - 2 * bit * lax.rem(lax.div(self.z, bit), 2)

    def z_mask(self, mask):
        out = self.z
        bit = 1
        while bit < self.nz:
            if mask & bit:
                out = out + bit - 2 * bit * lax.rem(lax.div(self.z, bit), 2)
            bit *= 2
        return out

    def neighbours(self):
        out = [self.at(a=1 - self.a), self.at(c=1 - self.c)]
        out += [self.at(b=self.b_off(i)) for i in range(1, self.nb)]
        out += [self.at(z=self.z_off(i)) for i in range(1, self.nz)]
        return out


def greet(targets):
    barrier = pltpu.get_barrier_semaphore()
    for target in targets:
        pl.semaphore_signal(barrier, inc=1, device_id=target, device_id_type=MESH)
    pl.semaphore_wait(barrier, len(targets))


class Sems:
    def __init__(self, send, recv):
        self.send, self.recv, self.used = send, recv, 0

    def copy(self, src, dst, target):
        i = self.used
        self.used += 1
        return pltpu.make_async_remote_copy(
            src_ref=src,
            dst_ref=dst,
            send_sem=self.send.at[i],
            recv_sem=self.recv.at[i],
            device_id=target,
            device_id_type=MESH,
        )


def start_all(copies):
    for copy in copies:
        copy.start()


def recv_all(copies):
    for copy in copies:
        copy.wait_recv()


def send_done(copies):
    for copy in copies:
        copy.wait_send()


def add_all(terms):
    if len(terms) == 2:
        return terms[0] + terms[1]
    return sum(t.astype(F32) for t in terms).astype(terms[0].dtype)


def gather_copies(nb, nz):
    return (nz - 1) + 1 + (nb - 1) + (nb - 1) + 1 + 1


class GatherPiece:
    def __init__(self, spot, sems, local_sem, src, out):
        a, b, c, z = spot.a, spot.b, spot.c, spot.z
        rows, width = src.shape
        half = rows // 2
        own = pl.ds(pl.multiple_of(z * width, LANES), width)
        top, low = pl.ds(0, half), pl.ds(half, half)
        mine = out.at[a, b, c, :, own]
        self.local = pltpu.make_async_copy(src, mine, local_sem)
        self.phases = [[sems.copy(src, mine, spot.at(z=spot.z_off(i))) for i in range(1, spot.nz)]]
        self.along = len(self.phases)
        self.phases += [
            [sems.copy(out.at[a, b, c, top], out.at[a, b, c, top], spot.at(a=1 - a))]
            + [
                sems.copy(out.at[a, b, c, low], out.at[a, b, c, low], spot.at(b=spot.b_off(i)))
                for i in range(1, spot.nb)
            ],
            [
                sems.copy(out.at[:, b, c, top], out.at[:, b, c, top], spot.at(b=spot.b_off(i)))
                for i in range(1, spot.nb)
            ]
            + [sems.copy(out.at[a, :, c, low], out.at[a, :, c, low], spot.at(a=1 - a))],
            [sems.copy(out.at[:, :, c], out.at[:, :, c], spot.at(c=1 - c))],
        ]

    def start(self, p):
        if p == 0:
            self.local.start()
        if p == self.along:
            self.local.wait()
        start_all(self.phases[p])

    def arrive(self, p):
        recv_all(self.phases[p])

    def close(self):
        for phase in self.phases:
            send_done(phase)


class Swap:
    def __init__(self, spot, sems, local_sem, src, dst):
        devices = spot.groups * spot.nz
        me = spot.g * spot.nz + spot.z
        self.local = pltpu.make_async_copy(src.at[me], dst.at[me], local_sem)
        self.copies = []
        for i in range(1, devices):
            other = lax.rem(me + i, devices)
            self.copies.append(
                sems.copy(src.at[other], dst.at[me], (lax.div(other, spot.nz), lax.rem(other, spot.nz)))
            )

    def start(self, part, parts):
        if part == 0:
            self.local.start()
        n = len(self.copies)
        start_all(self.copies[part * n // parts : (part + 1) * n // parts])

    def finish(self):
        self.local.wait()
        recv_all(self.copies)
        send_done(self.copies)


def timeline(pieces, times):
    phases = len(pieces[0].phases)
    steps = {}
    for t in reversed(range(len(pieces))):
        for p in range(phases + 1):
            steps.setdefault(times[t][p], []).append((t, p))

    def run(events):
        for t, p in events:
            if p > 0:
                pieces[t].arrive(p - 1)
            if p < phases:
                pieces[t].start(p)
            else:
                pieces[t].close()

    return {s: (lambda events=events: run(events)) for s, events in steps.items()}


class Ticks:
    def __init__(self, per):
        self.per, self.actions = per, {}

    def add(self, tick, action):
        self.actions.setdefault(tick, []).append(action)

    def add_all(self, actions):
        for tick, action in actions.items():
            self.add(tick, action)

    def here(self, c, first, last):
        for tick in sorted(self.actions):
            if tick % self.per == c and first <= tick // self.per <= last:

                @pl.when(pl.program_id(0) == tick // self.per)
                def _(mine=self.actions[tick]):
                    for action in mine:
                        action()


def during(first, last):
    return pl.when(jnp.logical_and(pl.program_id(0) >= first, pl.program_id(0) <= last))


def in_chunks(span, body):
    def step(i, carry):
        body(pl.ds(pl.multiple_of(i * ROWS, ROWS), ROWS))
        return carry

    lax.fori_loop(0, span // ROWS, step, 0)


def reduce_copies(nb, nz):
    return 1 + (nb - 1) + 1 + 1 + (nb - 1) + (nz - 1)


class ReducePiece:
    def __init__(self, spot, sems, local_sem, src, width, boxes, finish):
        self.spot, self.finish, self.width = spot, finish, width
        tile, self.r0, self.r1b, self.r1a, self.r2a, self.r2b, self.r3 = boxes
        a, b, c, z = spot.a, spot.b, spot.c, spot.z
        self.acc = acc = tile.at[:, :, c] if src is None else tile.at[:, :, 0]
        other = (tile if src is None else src).at[:, :, 1 - c]
        half = tile.shape[-2] // 2
        self.half = half
        top, low = pl.ds(0, half), pl.ds(half, half)
        self.local = None if src is None else pltpu.make_async_copy(src.at[:, :, c], acc, local_sem)
        columns = lambda zz: pl.ds(pl.multiple_of(zz * self.width, LANES), self.width)
        self.phases = [
            [sems.copy(other, self.r0, spot.at(c=1 - c))],
            [
                sems.copy(acc.at[:, spot.b_off(i), top], self.r1b.at[i - 1], spot.at(b=spot.b_off(i)))
                for i in range(1, spot.nb)
            ]
            + [sems.copy(acc.at[1 - a, :, low], self.r1a, spot.at(a=1 - a))],
            [sems.copy(acc.at[1 - a, b, top], self.r2a, spot.at(a=1 - a))]
            + [
                sems.copy(acc.at[a, spot.b_off(i), low], self.r2b.at[i - 1], spot.at(b=spot.b_off(i)))
                for i in range(1, spot.nb)
            ],
        ]
        self.columns = columns
        self.landed = []
        bit, slot = 1, 0
        while bit < spot.nz:
            masks = [m for m in range(spot.nz) if m & bit and m % bit == 0]
            target = spot.at(z=spot.z_flip(bit))
            self.phases.append(
                [
                    sems.copy(acc.at[a, b, :, columns(spot.z_mask(m))], self.r3.at[slot + i], target)
                    for i, m in enumerate(masks)
                ]
            )
            self.landed.append([(m ^ bit, slot + i) for i, m in enumerate(masks)])
            slot += len(masks)
            bit *= 2

    def start(self, p):
        if p == 0 and self.local is not None:
            self.local.start()
        start_all(self.phases[p])

    def arrive(self, p):
        spot, acc = self.spot, self.acc
        a, b = spot.a, spot.b
        top, low = pl.ds(0, self.half), pl.ds(self.half, self.half)
        recv_all(self.phases[p])
        if p == 0:
            if self.local is not None:
                self.local.wait()
            for i in range(2):
                for j in range(spot.nb):
                    acc[i, j] = acc[i, j] + self.r0[i, j]
        if p == 1:
            for i in range(2):
                acc[i, b, top] = add_all([acc[i, b, top]] + [self.r1b[k, i] for k in range(spot.nb - 1)])
            for j in range(spot.nb):
                acc[a, j, low] = acc[a, j, low] + self.r1a[j]
        if p == 2:
            acc[a, b, top] = acc[a, b, top] + self.r2a[...]
            acc[a, b, low] = add_all([acc[a, b, low]] + [self.r2b[k] for k in range(spot.nb - 1)])
        if p >= 3:
            for mask, slot in self.landed[p - 3]:
                block = self.columns(spot.z_mask(mask))
                if p == len(self.phases) - 1:
                    self.finish(acc[a, b, :, block].astype(F32) + self.r3[slot].astype(F32))
                else:
                    acc[a, b, :, block] = acc[a, b, :, block] + self.r3[slot]

    def close(self):
        for phase in self.phases:
            send_done(phase)


def reduce_boxes(nb, nz, rows, columns):
    half = rows // 2
    return [
        pltpu.VMEM((2, nb, 2, rows, columns), BF),
        pltpu.VMEM((2, nb, rows, columns), BF),
        pltpu.VMEM((nb - 1, 2, half, columns), BF),
        pltpu.VMEM((nb, half, columns), BF),
        pltpu.VMEM((half, columns), BF),
        pltpu.VMEM((nb - 1, half, columns), BF),
        pltpu.VMEM((nz - 1, rows, columns // nz), BF),
    ]


def key_parts(span, block):
    low = max(0, (block - 1) * ROWS)
    high = min(span, (block + 2) * ROWS)
    if low <= ROWS:
        return [(0, high)]
    return [(0, ROWS), (low, high)]


def head_masks():
    lane = lax.broadcasted_iota(jnp.int32, (1, LANES), 1)
    return (lane < HD, lane >= HD)


def only(mask, block):
    return jnp.where(mask, block, jnp.zeros_like(block))


def make_bias(marks_ref, bias):
    span = bias.shape[0]
    for i in range(0, span, ROWS):
        part = slice(i, i + ROWS)
        distance = lax.broadcasted_iota(jnp.int32, (ROWS, span), 0) + i - lax.broadcasted_iota(jnp.int32, (ROWS, span), 1)
        near = jnp.where(jnp.abs(distance) <= W // 2, 0.0, NEGATIVE)
        near = jnp.where(marks_ref[part, 1:2] > 0.5, 0.0, near)
        bias[part, :] = jnp.where(marks_ref[part, 0:1] > 0.5, near, NEGATIVE)


def attend_local(refs, bias_ref, a_ref, lse_ref, tick):
    k_ref, v_ref, q_ref = refs
    span = q_ref.shape[0]
    masks = head_masks()
    query = q_ref[...] * jnp.asarray(HD ** (-0.5), BF)
    values_flip = v_ref[...].T
    for block in range(span // ROWS):
        tick(block)
        rows = slice(block * ROWS, (block + 1) * ROWS)
        parts = key_parts(span, block)
        flips = []
        for h in range(2):
            head_query = only(masks[h], query[rows])
            scored = [
                product_back(k_ref[lo:hi, :], head_query) + bias_ref[lo:hi, rows] for lo, hi in parts
            ]
            top = jnp.max(scored[0], axis=0, keepdims=True)
            for s in scored[1:]:
                top = jnp.maximum(top, jnp.max(s, axis=0, keepdims=True))
            weights = [jnp.exp(s - top) for s in scored]
            total = sum(jnp.sum(w, axis=0, keepdims=True) for w in weights)
            lse_ref[0, h : h + 1, rows] = top + jnp.log(total)
            mixed = sum(
                product(values_flip[h * HD : (h + 1) * HD, lo:hi], w.astype(BF))
                for (lo, hi), w in zip(parts, weights)
            )
            flips.append(mixed * (1.0 / total))
        a_ref[rows, :] = jnp.concatenate(flips, axis=0).T.astype(BF)


def attend_global(refs, qg_ref, marks_ref, place_ref, a_ref, lse_global_ref):
    kg_ref, vg_ref = refs
    masks = head_masks()
    query = qg_ref[...] * jnp.asarray(HD ** (-0.5), BF)
    stacked = jnp.concatenate([only(m, query) for m in masks], axis=0)
    scores = product_back(kg_ref[...], stacked) + jnp.where(marks_ref[:, 0:1] > 0.5, 0.0, NEGATIVE)
    top = jnp.max(scores, axis=0, keepdims=True)
    probs = jnp.exp(scores - top)
    total = jnp.sum(probs, axis=0, keepdims=True)
    lse_global_ref[...] = jnp.broadcast_to(top + jnp.log(total), (8, LANES))
    probs = (probs * (1.0 / total)).astype(BF)
    mixed = product_left(probs, vg_ref[...])
    global_out = jnp.where(masks[0], mixed[:NG], mixed[NG:]).astype(BF)
    global_rows = product(place_ref[...], global_out)
    is_global = marks_ref[:ROWS, 1:2] > 0.5
    a_ref[:ROWS, :] = jnp.where(is_global, global_rows, a_ref[:ROWS, :].astype(F32)).astype(BF)


def attention_backward(refs, qg_ref, bias_ref, marks_ref, place_ref, a_ref, da_ref, lse_ref, lse_global_ref,
                       back_refs, dqg_ref, sums_ref, dk_sum, dv_sum, tick):
    k_ref, v_ref, q_ref, kg_ref, vg_ref = refs
    dk_ref, dv_ref, dq_ref, dkg_ref, dvg_ref = back_refs
    span = q_ref.shape[0]
    masks = head_masks()
    scale = HD ** (-0.5)
    query = q_ref[...] * jnp.asarray(scale, BF)
    keys_flip = k_ref[...].T
    query_global = qg_ref[...] * jnp.asarray(scale, BF)
    stacked = jnp.concatenate([only(m, query_global) for m in masks], axis=0)
    adjoint_global = product_left(place_ref[...], da_ref[:ROWS, :]).astype(BF)
    adjoint_stacked = jnp.concatenate([only(m, adjoint_global) for m in masks], axis=0)
    scores = product_back(kg_ref[...], stacked) + jnp.where(marks_ref[:, 0:1] > 0.5, 0.0, NEGATIVE)
    probs = jnp.exp(scores - lse_global_ref[0, 0:1, :])
    prob_adjoint = product_back(vg_ref[...], adjoint_stacked)
    center = jnp.sum(probs * prob_adjoint, axis=0, keepdims=True)
    score_adjoint = (probs * (prob_adjoint - center)).astype(BF)
    mixed = product_left(score_adjoint, kg_ref[...]) * scale
    dqg_ref[...] = jnp.where(masks[0], mixed[:NG], mixed[NG:]).astype(BF)
    dkg_ref[...] = product(score_adjoint, stacked).astype(BF)
    dvg_ref[...] = product(probs.astype(BF), adjoint_stacked).astype(BF)
    first = jnp.where(marks_ref[:ROWS, 1:2] > 0.5, 0.0, da_ref[:ROWS, :].astype(F32)).astype(BF)
    adjoint = jnp.concatenate([first, da_ref[ROWS:, :]], axis=0)
    inner = adjoint.astype(F32) * a_ref[...].astype(F32)
    picker = (lax.broadcasted_iota(jnp.int32, (8, LANES), 0) == lax.div(lax.broadcasted_iota(jnp.int32, (8, LANES), 1), HD)).astype(F32)
    centers = lax.dot_general(
        picker, inner, (((1,), (1,)), ((), ())), preferred_element_type=F32, precision=lax.Precision.HIGHEST
    )
    dk_sum[...] = jnp.zeros_like(dk_sum)
    dv_sum[...] = jnp.zeros_like(dv_sum)
    for block in range(span // ROWS):
        tick(block)
        rows = slice(block * ROWS, (block + 1) * ROWS)
        parts = key_parts(span, block)
        flips = []
        for h in range(2):
            head_query = only(masks[h], query[rows])
            head_adjoint = only(masks[h], adjoint[rows])
            log_sum = lse_ref[0, h : h + 1, rows]
            center = centers[h : h + 1, rows]
            mixed = None
            for lo, hi in parts:
                s = product_back(k_ref[lo:hi, :], head_query) + bias_ref[lo:hi, rows]
                weights = jnp.exp(s - log_sum)
                prob_adjoint = product_back(v_ref[lo:hi, :], head_adjoint)
                score_adjoint = (weights * (prob_adjoint - center)).astype(BF)
                dv_sum[lo:hi, :] += product(weights.astype(BF), head_adjoint)
                dk_sum[lo:hi, :] += product(score_adjoint, head_query)
                part = product(keys_flip[h * HD : (h + 1) * HD, lo:hi], score_adjoint)
                mixed = part if mixed is None else mixed + part
            flips.append(mixed)
        dq_ref[rows, :] = (jnp.concatenate(flips, axis=0).T * scale).astype(BF)
    dk_ref[...] = dk_sum[...].astype(BF)
    dv_ref[...] = dv_sum[...].astype(BF)
    sums = [jnp.sum(r[...].astype(F32), axis=0, keepdims=True) for r in (dq_ref, dv_ref, dqg_ref, dvg_ref)]
    sums_ref[...] = jnp.concatenate(sums + [jnp.zeros((4, LANES), F32)], axis=0)


def gelu_and_slope(u):
    e = jnp.exp2(u * (u * (-0.5 * 1.4426950408889634)))
    t = 1.0 / (1.0 + (0.3275911 * 0.7071067811865476) * jnp.abs(u))
    tail = 0.5 * -1.453152027 + t * (0.5 * 1.061405429)
    tail = 0.5 * -0.284496736 + t * (0.5 * 1.421413741 + t * tail)
    tail = t * (0.5 * 0.254829592 + t * tail) * e
    phi = jnp.where(u >= 0.0, 1.0 - tail, tail)
    return u * phi, phi + u * e * 0.3989422804014327


def normalize(mixture):
    centered = mixture - jnp.mean(mixture, axis=-1, keepdims=True)
    spread = lax.rsqrt(jnp.mean(centered * centered, axis=-1, keepdims=True) + EPS_NORM)
    return centered * spread, spread


def normalize_back(adjoint, normal, spread, gain):
    scaled = adjoint * gain
    mean = jnp.mean(scaled, axis=-1, keepdims=True)
    along = jnp.mean(scaled * normal, axis=-1, keepdims=True)
    return spread * (scaled - mean - normal * along)


def kernel_params(collective=None, **more):
    if collective is not None:
        more.update(collective_id=collective, has_side_effects=True)
    return pltpu.CompilerParams(vmem_limit_bytes=61 * MIB, **more)


def dma(count):
    return pltpu.SemaphoreType.DMA((count,))


def still(*shape):
    return pl.BlockSpec(shape, lambda s: (0,) * len(shape), pipeline_mode=pl.Buffered(1))


def full_shape(nb, block, columns, *lead):
    return lead + (2, nb, 2, block, columns)


def everyone(spot):
    devices = spot.groups * spot.nz
    me = spot.g * spot.nz + spot.z
    ids = [lax.rem(me + i, devices) for i in range(1, devices)]
    return [(lax.div(i, spot.nz), lax.rem(i, spot.nz)) for i in ids]


def project_and_attend(mesh, low_in, low_rest, low_vectors, sequence, places, lengths, parts):
    groups, depth = mesh.shape["grp"], mesh.shape["dp"]
    nb = groups // 4
    count, block, width = low_in.shape
    rest = low_rest.shape[0]
    span, columns = sequence.shape
    devices = groups * depth
    few = places.shape[1]
    pairs = H // 2
    total = (count + rest) * gather_copies(nb, depth) + depth - 1 + devices - 1
    lag = 3
    local_count = 3
    attend = lag + local_count
    project = attend + pairs
    glob = project + count - local_count
    together = 2
    steps = glob + pairs // together

    def slot(s):
        return 4 * s if s < attend else 4 * attend + 6 * (s - attend)

    def kernel(in_ref, rest_ref, vec_ref, seq_ref, places_ref, lengths_ref, part_ref,
               full_ref, out_ref, up_ref, vec_full_ref, proj_ref, few_ref, a_ref, lse_ref, lse_global_ref, swapped_ref,
               marks_ref, place_ref, vec_out_ref,
               weight, vec, proj, bias, send, recv, local):
        spot = Spot(groups, depth)
        sems = Sems(send, recv)
        pairs_of = [(in_ref.at[t], full_ref.at[t]) for t in range(count)]
        pairs_of += [(rest_ref.at[0], out_ref)] + [(rest_ref.at[1 + q], up_ref.at[q]) for q in range(rest - 1)]
        pieces = [GatherPiece(spot, sems, local.at[t], src, out) for t, (src, out) in enumerate(pairs_of)]
        swap = Swap(spot, sems, local.at[count + rest], part_ref, swapped_ref)
        own = pl.ds(pl.multiple_of(spot.z * width, LANES), width)
        mine = vec_full_ref.at[:, own]
        vec_local = pltpu.make_async_copy(vec_ref, mine, local.at[count + rest + 1])
        vec_sends = [sems.copy(vec_ref, mine, spot.at(z=spot.z_off(i))) for i in range(1, depth)]
        keep = [
            pltpu.make_async_copy(proj.at[t], proj_ref.at[t], local.at[count + rest + 2 + t]) for t in range(count - 1)
        ]
        step = pl.program_id(0)
        ticks = Ticks(4)
        times = []
        for t in range(count + rest):
            if t < local_count:
                times.append([max(0, slot(t - 1) + 1), slot(t), slot(t + 1) + 1, slot(t + 2) + 2, slot(t + 3) + 3])
            else:
                times.append([slot(t - 2) + 1, slot(t), slot(t + 2) + 1, slot(t + 4) + 2, slot(t + 5) + 3])
        ticks.add_all(timeline(pieces, times))
        for j in range(8):
            ticks.add(4 * (attend + 2 * j if j < 4 else project + j - 4) + 2, lambda j=j: swap.start(j, 8))

        @pl.when(step == 0)
        def _():
            greet(everyone(spot))
            vec_local.start()
            start_all(vec_sends)

        for c in range(4):
            ticks.here(c, 0, attend - 1)

        @pl.when(step == 0)
        def _():
            me = spot.g * depth + spot.z
            spots = places_ref[pl.ds(me, 1), :]
            length = lengths_ref[pl.ds(me, 1), :]
            for i in range(0, span, ROWS):
                hit = (lax.broadcasted_iota(jnp.int32, (ROWS, few), 0) + i == spots).astype(F32)
                if i == 0:
                    place_ref[...] = hit.astype(BF)
                is_global = jnp.max(hit, axis=1, keepdims=True)
                lane = lax.broadcasted_iota(jnp.int32, (ROWS, LANES), 1)
                valid = (lax.broadcasted_iota(jnp.int32, (ROWS, LANES), 0) + i < length).astype(F32)
                marks_ref[i : i + ROWS, :] = jnp.where(lane == 0, valid, jnp.where(lane == 1, is_global, 0.0))
            make_bias(marks_ref, bias)

        @pl.when(step == lag)
        def _():
            vec_local.wait()
            recv_all(vec_sends)
            send_done(vec_sends)
            pltpu.sync_copy(vec_full_ref, vec)
            vec_out_ref[...] = vec[...].astype(F32)

        def offset(row):
            index = lax.broadcasted_iota(jnp.int32, vec.shape, 0)
            return jnp.sum(jnp.where(index == row, vec[...].astype(F32), 0.0), axis=0, keepdims=True)

        for c in range(4):
            ticks.here(c, project, steps - 1)

        def project_one(t):
            pltpu.sync_copy(full_ref.at[t], weight)
            added = offset(jnp.where(t == 1, 1, jnp.where(t == 2, 0, jnp.where(t == 4, 4, 15))))

            def body(rows):
                matrix = weight[...].reshape(groups * block, columns)
                proj[t, rows, :] = (product(seq_ref[rows, :], matrix) + added).astype(BF)

            in_chunks(span, body)

        first_part = jnp.logical_and(step >= lag, step < attend)
        second_part = jnp.logical_and(step >= project, step < glob - 1)
        pl.when(jnp.logical_or(first_part, second_part))(
            lambda: project_one(jnp.where(step < attend, step - lag, step - project + local_count))
        )
        for t in range(count - 1):
            pl.when(step == (lag + t if t < local_count else project + t - local_count))(keep[t].start)

        @pl.when(step == glob - 1)
        def _():
            pltpu.sync_copy(full_ref.at[count - 1], weight)
            matrix = weight[...].reshape(groups * block, columns)
            rows = product_left(place_ref[...], seq_ref[:ROWS, :]).astype(BF)
            few_ref[...] = (product(rows, matrix) + offset(3)).astype(BF)

        @during(attend, project - 1)
        def _():
            lanes = pl.ds(pl.multiple_of((step - attend) * LANES, LANES), LANES)
            attend_local(
                [proj.at[i, :, lanes] for i in range(local_count)], bias, a_ref.at[:, lanes], lse_ref,
                lambda c: ticks.here(c, attend, project - 1),
            )

        @pl.when(step >= glob)
        def _():
            def one(i, carry):
                pair = (step - glob) * together + i
                lanes = pl.ds(pl.multiple_of(pair * LANES, LANES), LANES)
                attend_global(
                    [proj.at[i, :, lanes] for i in range(local_count, count - 1)], few_ref.at[:, lanes], marks_ref, place_ref,
                    a_ref.at[:, lanes], lse_global_ref.at[pair],
                )
                return carry

            lax.fori_loop(0, together, one, 0)

        @pl.when(step == steps - 1)
        def _():
            for copy in keep:
                copy.wait()
            swap.finish()

    at = lambda s: jnp.clip(s - attend, 0, pairs - 1)
    results = pl.pallas_call(
        kernel,
        grid=(steps,),
        in_specs=[ANYSPEC] * 3 + [still(span, columns), still(*places.shape), still(*lengths.shape), ANYSPEC],
        out_specs=[ANYSPEC] * 5
        + [
            pl.BlockSpec((few, columns), lambda s: (0, 0)),
            pl.BlockSpec((span, columns), lambda s: (0, 0)),
            pl.BlockSpec((1, 8, span), lambda s: (at(s), 0, 0)),
            pl.BlockSpec((pairs, 8, LANES), lambda s: (0, 0, 0)),
            ANYSPEC,
            pl.BlockSpec((span, LANES), lambda s: (0, 0)),
            pl.BlockSpec((ROWS, few), lambda s: (0, 0)),
            pl.BlockSpec((low_vectors.shape[0], columns), lambda s: (0, 0)),
        ],
        out_shape=[
            jax.ShapeDtypeStruct(full_shape(nb, block, columns, count), BF),
            jax.ShapeDtypeStruct(full_shape(nb, block, columns), BF),
            jax.ShapeDtypeStruct(full_shape(nb, block, columns, rest - 1), BF),
            jax.ShapeDtypeStruct((low_vectors.shape[0], columns), BF),
            jax.ShapeDtypeStruct((count - 1, span, columns), BF),
            jax.ShapeDtypeStruct((few, columns), BF),
            jax.ShapeDtypeStruct((span, columns), BF),
            jax.ShapeDtypeStruct((pairs, 8, span), F32),
            jax.ShapeDtypeStruct((pairs, 8, LANES), F32),
            jax.ShapeDtypeStruct(parts.shape, BF),
            jax.ShapeDtypeStruct((span, LANES), F32),
            jax.ShapeDtypeStruct((ROWS, few), BF),
            jax.ShapeDtypeStruct((low_vectors.shape[0], columns), F32),
        ],
        scratch_shapes=[
            pltpu.VMEM(full_shape(nb, block, columns), BF),
            pltpu.VMEM((low_vectors.shape[0], columns), BF),
            pltpu.VMEM((count - 1, span, columns), BF),
            pltpu.VMEM((span, span), F32),
            dma(total),
            dma(total),
            dma(count + rest + 2 + count - 1),
        ],
        compiler_params=kernel_params(0),
        name="project_and_attend",
    )(low_in, low_rest, low_vectors, sequence, places, lengths, parts)
    square = (groups * block, columns)
    full_in, full_out, full_up = results[:3]
    return (full_in.reshape((count,) + square), full_out.reshape(square), full_up.reshape((rest - 1,) + square)) + tuple(
        results[3:]
    )


def feed_forward(mesh, sequence, attended, full_out, full_up, shards, parts, vectors, hidden_bias, valid):
    groups, depth = mesh.shape["grp"], mesh.shape["dp"]
    nb = groups // 4
    span, columns = sequence.shape
    count, block, width = shards.shape
    devices = groups * depth
    total = count * gather_copies(nb, depth) + devices - 1
    steps = count + 3
    extra = FF // D

    def kernel(seq_ref, att_ref, wo_ref, up_ref, shard_ref, part_ref, vec_ref, hb_ref, valid_ref,
               full_ref, hid_ref, slope_ref, low_ref, normal_ref, spread_ref, layer_ref, feed_low_ref, sum_ref, sums_ref,
               first, low, normal, hidden, feed, weight, cot, send, recv, local):
        spot = Spot(groups, depth)
        sems = Sems(send, recv)
        pieces = [GatherPiece(spot, sems, local.at[t], shard_ref.at[t], full_ref.at[t]) for t in range(count)]
        swap = Swap(spot, sems, local.at[count], part_ref, cot)
        keep_low = pltpu.make_async_copy(low, low_ref, local.at[count + 1])
        keep_normal = pltpu.make_async_copy(normal, normal_ref, local.at[count + 2])
        keep_hidden = [
            pltpu.make_async_copy(hidden.at[q], hid_ref.at[q], local.at[count + 3 + q]) for q in range(count)
        ]
        keep_sum = pltpu.make_async_copy(feed, sum_ref, local.at[2 * count + 3])
        step = pl.program_id(0)

        @pl.when(step == 0)
        def _():
            greet(everyone(spot))

        ticks = Ticks(8)
        starts = [[0, 1, 2, 3], [8, 16, 24, 32], [10, 19, 28, 37], [18, 27, 36, 45], [25, 34, 44, 52]]
        ticks.add_all(timeline(pieces, [[row[q] for row in starts] for q in range(count)]))
        for j, tick in enumerate((3, 5, 8, 9, 10, 11, 16, 17)):
            ticks.add(tick, lambda j=j: swap.start(j, 8))
        chunks = [slice(i, i + ROWS) for i in range(0, span, ROWS)]

        def work(first, last, offset, body):
            @during(first, last)
            def _():
                for c, rows in enumerate(chunks):
                    ticks.here(offset + c, first, last)
                    body(rows)

        def idle(first, last, offset):
            for c in range(len(chunks)):
                ticks.here(offset + c, first, last)

        def norm(rows):
            mixture = seq_ref[rows, :].astype(F32) + product(att_ref[rows, :], wo_ref[...]) + vec_ref[2:3, :]
            centered, spread = normalize(mixture)
            out = centered * vec_ref[6 + extra : 7 + extra, :] + vec_ref[7 + extra : 8 + extra, :]
            first[rows, :] = out
            low[rows, :] = out.astype(BF)
            feed[rows, :] = jnp.broadcast_to(vec_ref[5 + extra : 6 + extra, :], (ROWS, columns))
            normal[rows, :] = centered.astype(BF)
            spread_ref[rows, :] = jnp.broadcast_to(spread, (ROWS, LANES))

        def up(rows):
            q = step - 1
            u = product(low[rows, :], up_ref[0]) + hb_ref[pl.ds(q, 1), :]
            act, slope = gelu_and_slope(u)
            hidden[q, rows, :] = act.astype(BF)
            slope_ref[0, rows, :] = slope.astype(BF)

        def down(rows):
            part = product(hidden[step - 3, rows, :], weight[...].reshape(groups * block, columns))
            feed[rows, :] += part

        work(0, 0, 0, norm)

        @pl.when(step == 0)
        def _():
            keep_low.start()
            keep_normal.start()

        idle(0, 2, 4)
        work(1, count, 0, up)
        for q in range(count):
            pl.when(step == q + 1)(keep_hidden[q].start)
        idle(count + 1, steps - 1, 0)
        for q in range(count):

            @pl.when(step == q + 3)
            def _(q=q):
                ticks.here(4, q + 3, q + 3)
                pltpu.sync_copy(full_ref.at[q], weight)

        @during(3, steps - 1)
        def _():
            for c, rows in enumerate(chunks):
                if c:
                    ticks.here(4 + c, 3, steps - 1)
                down(rows)


        @pl.when(step == steps - 1)
        def _():
            swap.finish()
            sums_ref[...] = jnp.zeros_like(sums_ref)
            pieces_of = span // devices

            def body(rows):
                part = pl.ds(rows.start // pieces_of, ROWS // pieces_of)
                mask = valid_ref[rows, 0:1]
                cotangent = cot[part].reshape(ROWS, columns).astype(F32) * mask
                gain = vec_ref[8 + extra : 9 + extra, :]
                mixture = first[rows, :] + feed[rows, :]
                centered, spread = normalize(mixture)
                layer_ref[rows, :] = ((centered * gain + vec_ref[9 + extra : 10 + extra, :]) * mask).astype(BF)
                back = normalize_back(cotangent, centered, spread, gain)
                back_low = back.astype(BF)
                feed[rows, :] = back
                feed_low_ref[rows, :] = back_low
                sums_ref[0:1, :] += jnp.sum(back_low.astype(F32), axis=0, keepdims=True)
                sums_ref[1:2, :] += jnp.sum(cotangent * centered, axis=0, keepdims=True)
                sums_ref[2:3, :] += jnp.sum(cotangent, axis=0, keepdims=True)

            in_chunks(span, body)
            keep_sum.start()
            keep_low.wait()
            keep_normal.wait()
            for copy in keep_hidden:
                copy.wait()
            keep_sum.wait()

    matrix = lambda kind: jax.ShapeDtypeStruct((span, columns), kind)
    stack = jax.ShapeDtypeStruct((count, span, columns), BF)
    by_q = pl.BlockSpec((1, span, columns), lambda s: (jnp.clip(s - 1, 0, count - 1), 0, 0))
    results = pl.pallas_call(
        kernel,
        grid=(steps,),
        in_specs=[
            still(span, columns), still(span, columns), still(*full_out.shape), by_q, ANYSPEC, ANYSPEC,
            still(*vectors.shape), still(*hidden_bias.shape), still(*valid.shape),
        ],
        out_specs=[ANYSPEC, ANYSPEC, by_q, ANYSPEC, ANYSPEC]
        + [pl.BlockSpec((span, LANES), lambda s: (0, 0))]
        + [pl.BlockSpec((span, columns), lambda s: (0, 0))] * 2
        + [ANYSPEC, pl.BlockSpec((8, columns), lambda s: (0, 0))],
        out_shape=[
            jax.ShapeDtypeStruct(full_shape(nb, block, columns, count), BF), stack, stack, matrix(BF), matrix(BF),
            jax.ShapeDtypeStruct((span, LANES), F32), matrix(BF), matrix(BF), matrix(F32),
            jax.ShapeDtypeStruct((8, columns), F32),
        ],
        scratch_shapes=[
            pltpu.VMEM((span, columns), F32),
            pltpu.VMEM((span, columns), BF),
            pltpu.VMEM((span, columns), BF),
            pltpu.VMEM((count, span, columns), BF),
            pltpu.VMEM((span, columns), F32),
            pltpu.VMEM(full_shape(nb, block, columns), BF),
            pltpu.VMEM(parts.shape, BF),
            dma(total),
            dma(total),
            dma(2 * count + 4),
        ],
        compiler_params=kernel_params(1),
        name="feed_forward",
    )(sequence, attended, full_out, full_up, shards, parts, vectors, hidden_bias, valid)
    return (results[0].reshape(count, groups * block, columns),) + tuple(results[1:])


def feed_backward(mesh, feed_low, low, hidden, slope, full_up, full_down, sum_adjoint, attended, full_out, normal, spread,
                  gain, parts):
    groups, depth = mesh.shape["grp"], mesh.shape["dp"]
    nb = groups // 4
    span, columns = feed_low.shape
    count = hidden.shape[0]
    block, width = columns // groups, columns // depth
    devices = groups * depth
    half = columns // 2
    total = count * reduce_copies(nb, depth) + devices - 1
    work = 3 * count
    steps = work + 2
    boxes = [reduce_boxes(nb, depth, block, columns) for _ in range(count)]
    per = len(boxes[0])

    def kernel(feed_ref, low_ref, hid_ref, slope_ref, up_ref, down_ref, sum_ref, att_ref, wo_ref, normal_ref, spread_ref,
               gain_ref, part_ref,
               change_ref, hb_ref, mix_ref, own_ref, swapped_ref, out_change_ref, att_back_ref, sums_ref,
               back_low, norm, branch, send, recv, local, *box_refs):
        spot = Spot(groups, depth)
        sems = Sems(send, recv)
        tiles = [box_refs[q * per] for q in range(count)]

        def finish(q):
            def store(value):
                own_ref[q] = value

            return store

        pieces = [
            ReducePiece(spot, sems, None, None, width, box_refs[q * per : (q + 1) * per], finish(q)) for q in range(count)
        ]
        swap = Swap(spot, sems, local.at[0], part_ref, swapped_ref)
        keep = pltpu.make_async_copy(norm, mix_ref, local.at[1])
        fetch = pltpu.make_async_copy(sum_ref, norm, local.at[2])
        step = pl.program_id(0)
        ticks = Ticks(4)
        starts = [[3, 7, 11, 15], [7, 19, 27, 35], [17, 25, 33, 41], [22, 30, 38, 46]]
        starts += [[26, 34, 42, 50]] * (len(pieces[0].phases) - 4) + [[31, 39, 47, 54]]
        ticks.add_all(timeline(pieces, [[row[q] for row in starts] for q in range(count)]))
        for j in range(8):
            ticks.add(4 * (j + 2), lambda j=j: swap.start(j, 8))
        chunks = [slice(i, i + ROWS) for i in range(0, span, ROWS)]

        def work_on(first, last, body):
            for c, rows in enumerate(chunks):
                if c == len(chunks) // 2:
                    ticks.here(1, first, last)
                body(rows)
            ticks.here(2, first, last)

        @pl.when(step == 0)
        def _():
            greet(everyone(spot))
            fetch.start()

        ticks.here(0, 0, steps - 1)

        for q in range(count):

            @pl.when(step == q)
            def _(q=q):
                value = product_left(hid_ref[0], feed_ref[...]).astype(BF)
                tiles[q][...] = value.reshape(full_shape(nb, block, columns))

        pl.when(step == count)(fetch.wait)

        for c in (1, 2):
            ticks.here(c, 0, count - 1)

        @during(count, work - 1)
        def _():
            hb_ref[...] = jnp.zeros_like(hb_ref)

            def body(rows):
                value = product_back(feed_ref[rows, :], down_ref[0]) * slope_ref[0, rows, :].astype(F32)
                value = value.astype(BF)
                back_low[rows, :] = value
                hb_ref[0] += jnp.broadcast_to(jnp.sum(value.astype(F32), axis=0, keepdims=True), (8, half))
                norm[rows, :] += product_back(value, up_ref[0])

            work_on(count, work - 1, body)
            change_ref[0] = product_left(low_ref[...], back_low[...]).astype(BF)

        @pl.when(step == work)
        def _():
            sums_ref[...] = jnp.zeros_like(sums_ref)

            def body(rows):
                adjoint = norm[rows, :]
                centered = normal_ref[rows, :].astype(F32)
                back = normalize_back(adjoint, centered, spread_ref[rows, 0:1], gain_ref[6 + count : 7 + count, :])
                back_branch = back.astype(BF)
                norm[rows, :] = back
                branch[rows, :] = back_branch
                sums_ref[0:1, :] += jnp.sum(back_branch.astype(F32), axis=0, keepdims=True)
                sums_ref[1:2, :] += jnp.sum(adjoint * centered, axis=0, keepdims=True)
                sums_ref[2:3, :] += jnp.sum(adjoint, axis=0, keepdims=True)
                att_back_ref[rows, :] = product_back(back_branch, wo_ref[...]).astype(BF)

            work_on(work, work, body)
            keep.start()
            out_change_ref[...] = product_left(att_ref[...], branch[...]).astype(BF)

        ticks.here(3, 0, work)
        for c in range(1, 4):
            ticks.here(c, work + 1, steps - 1)

        @pl.when(step == steps - 1)
        def _():
            keep.wait()
            swap.finish()

    at = lambda s: jnp.clip(s - count, 0, 2 * count - 1)
    by_half = pl.BlockSpec((1, span, half), lambda s: (lax.div(at(s), 2), 0, lax.rem(at(s), 2)))
    whole = lambda *dims: pl.BlockSpec(dims, lambda s: (0,) * len(dims))
    return pl.pallas_call(
        kernel,
        grid=(steps,),
        in_specs=[
            still(span, columns), still(span, columns),
            pl.BlockSpec((1, span, columns), lambda s: (jnp.minimum(s, count - 1), 0, 0)),
            by_half, by_half,
            pl.BlockSpec((1, half, columns), lambda s: (lax.div(at(s), 2), lax.rem(at(s), 2), 0)),
            ANYSPEC, still(span, columns), still(columns, columns), still(span, columns), still(span, LANES),
            still(*gain.shape), ANYSPEC,
        ],
        out_specs=[
            by_half,
            pl.BlockSpec((1, 8, half), lambda s: (lax.div(at(s), 2), 0, lax.rem(at(s), 2))),
            ANYSPEC, whole(count, block, width), ANYSPEC, whole(columns, columns), whole(span, columns), whole(8, columns),
        ],
        out_shape=[
            jax.ShapeDtypeStruct((count, columns, columns), BF),
            jax.ShapeDtypeStruct((count, 8, columns), F32),
            jax.ShapeDtypeStruct((span, columns), F32),
            jax.ShapeDtypeStruct((count, block, width), F32),
            jax.ShapeDtypeStruct(parts.shape, BF),
            jax.ShapeDtypeStruct((columns, columns), BF),
            jax.ShapeDtypeStruct((span, columns), BF),
            jax.ShapeDtypeStruct((8, columns), F32),
        ],
        scratch_shapes=[
            pltpu.VMEM((span, half), BF),
            pltpu.VMEM((span, columns), F32),
            pltpu.VMEM((span, columns), BF),
            dma(total),
            dma(total),
            dma(3),
        ]
        + [box for some in boxes for box in some],
        compiler_params=kernel_params(2),
        name="feed_backward",
    )(feed_low, low, hidden, slope, full_up, full_down, sum_adjoint, attended, full_out, normal, spread, gain, parts)


def attend_back_and_reduce(mesh, projected, query_global, marks, place, attended, attended_adjoint, log_sums, log_sums_global,
                           changes, parts, full_in, sequence, mixture_adjoint, hidden_sums, feed_sums, norm_sums, order):
    groups, depth = mesh.shape["grp"], mesh.shape["dp"]
    nb = groups // 4
    span, columns = sequence.shape
    pairs = H // 2
    count = full_in.shape[0]
    few = query_global.shape[0]
    block, width = columns // groups, columns // depth
    devices = groups * depth
    views = [c.reshape((-1,) + full_shape(nb, block, columns)) for c in changes]
    where = [(i, t) for i, v in enumerate(views) for t in range(v.shape[0])]
    early = len(where)
    given = len(views)
    vec_rows = 16
    extra = hidden_sums.shape[0]
    total = (early + count) * reduce_copies(nb, depth) + devices - 1 + depth - 1 + groups - 1
    late_starts = [4 * (pairs + t) + 1 for t in range(count)]
    fresh = early - early // 2
    steps = (late_starts[-1] + 17) // 4 + 1
    boxes = [reduce_boxes(nb, depth, block, columns) for _ in range(early + fresh)]
    for i in range(count - fresh, early):
        boxes[i][0] = pltpu.VMEM((2, nb, 1, block, columns), BF)
    per = len(boxes[0])

    def kernel(*refs):
        stack_ref, few_ref, marks_ref, place_ref, a_ref, da_ref, lse_ref, lse_global_ref = refs[:8]
        change_refs, refs = refs[8 : 8 + given], refs[8 + given :]
        part_ref, weight_ref, seq_ref, mix_ref, hidden_ref, feed_ref, norm_ref = refs[:7]
        own_refs, own_in_ref, vec_out, grad_ref, swapped_ref = refs[7 : 7 + given], *refs[7 + given : 11 + given]
        refs = refs[11 + given :]
        bias, back, dqg, sums, dk_sum, dv_sum, grad, vec, vec_z, vec_g, send, recv, local, free = refs[:14]
        box_refs = refs[14:]
        spot = Spot(groups, depth)
        sems = Sems(send, recv)

        def finish(ref, i):
            def store(value):
                ref[i] = value

            return store

        box = lambda i: box_refs[i * per : (i + 1) * per]
        pieces = [
            ReducePiece(spot, sems, local.at[i], change_refs[v].at[t], width, box(i), finish(own_refs[v], t))
            for i, (v, t) in enumerate(where)
        ]
        late_box = list(range(early, early + fresh)) + list(range(count - fresh))
        late = [
            ReducePiece(spot, sems, None, None, width, box(late_box[t]), finish(own_in_ref, int(order[t]))) for t in range(count)
        ]
        tiles = [box_refs[late_box[t] * per] for t in range(count)]
        swap = Swap(spot, sems, local.at[early], part_ref, swapped_ref)
        fetch = pltpu.make_async_copy(mix_ref, grad, local.at[early + 1])
        keep = pltpu.make_async_copy(back.at[0], grad_ref, local.at[early + 2])
        part = lambda zz: pl.ds(pl.multiple_of(zz * width, LANES), width)
        first = [
            sems.copy(vec.at[:, part(spot.z_off(i))], vec_z.at[i - 1], spot.at(z=spot.z_off(i)))
            for i in range(1, depth)
        ]
        second = [
            sems.copy(vec_g.at[spot.g], vec_g.at[spot.g], (lax.rem(spot.g + i, groups), spot.z))
            for i in range(1, groups)
        ]
        step = pl.program_id(0)
        ticks = Ticks(4)
        more = len(pieces[0].phases) - 4
        ticks.add_all(
            timeline(
                pieces,
                [
                    [max(0, 6 * t - 4), 6 * t + 2, 6 * t + 10, 6 * t + 18] + [6 * t + 21] * more + [6 * t + 25]
                    for t in range(early)
                ],
            )
        )
        for j in range(4 * pairs - 1):
            ticks.add(1 + j, lambda j=j: swap.start(j, 4 * pairs - 1))

        def freed():
            for target in spot.neighbours():
                pl.semaphore_signal(free, inc=1, device_id=target, device_id_type=MESH)

        ticks.add(6 * (count - fresh - 1) + 25, freed)
        ticks.add(late_starts[fresh], lambda: pl.semaphore_wait(free, len(spot.neighbours())))
        late_times = [[m, m + 2, m + 7, m + 12] + [m + 14] * more + [m + 17] for m in late_starts]
        ticks.add_all(timeline(late, late_times))

        @pl.when(step == 0)
        def _():
            greet(everyone(spot))
            fetch.start()
            make_bias(marks_ref, bias)

        @pl.when(step < pairs)
        def _():
            lanes = pl.ds(pl.multiple_of(step * LANES, LANES), LANES)
            attention_backward(
                [stack_ref.at[i] for i in range(5)], few_ref, bias, marks_ref, place_ref,
                a_ref, da_ref, lse_ref, lse_global_ref,
                [back.at[i, :, lanes] for i in range(5)], dqg.at[:, lanes], sums.at[:, lanes], dk_sum, dv_sum,
                lambda c: ticks.here(c, 0, pairs - 1),
            )

        @pl.when(step == pairs)
        def _():
            fetch.wait()
            vec[...] = jnp.zeros_like(vec)
            vec[0:2, :] = sums[0:2, :]
            vec[2:3, :] = norm_ref[0:1, :]
            vec[3:5, :] = sums[2:4, :]
            vec[5 : 5 + extra, :] = hidden_ref[...]
            vec[5 + extra : 6 + extra, :] = feed_ref[0:1, :]
            vec[6 + extra : 8 + extra, :] = norm_ref[1:3, :]
            vec[8 + extra : 10 + extra, :] = feed_ref[1:3, :]
            start_all(first)

        ticks.here(0, pairs, steps - 1)

        for t in range(count - 1):

            @pl.when(step == pairs + t)
            def _(t=t):
                value = product_left(seq_ref[...], back[t]).astype(BF)
                tiles[t][...] = value.reshape(full_shape(nb, block, columns))

        @pl.when(step == pairs + count - 1)
        def _():
            rows = product_left(place_ref[...], seq_ref[:ROWS, :]).astype(BF)
            value = product_left(rows, dqg[...]).astype(BF)
            tiles[count - 1][...] = value.reshape(full_shape(nb, block, columns))

        ticks.here(1, pairs, steps - 1)

        def grad_rows(first_row, last_row):
            @during(pairs, pairs + count - 2)
            def _():
                for r in range(first_row, last_row, ROWS):
                    rows = slice(r, r + ROWS)
                    grad[rows, :] += product_back(back[step - pairs, rows, :], weight_ref[0])

        grad_rows(0, span // 2)
        ticks.here(2, pairs, steps - 1)
        grad_rows(span // 2, span)

        @pl.when(step == pairs + count - 1)
        def _():
            extra = product_back(dqg[...], weight_ref[0])
            grad[:ROWS, :] += lax.dot_general(
                place_ref[...].astype(F32), extra, (((1,), (0,)), ((), ())),
                precision=lax.Precision.HIGHEST, preferred_element_type=F32,
            )
            back[0] = grad[...].astype(BF)
            keep.start()

        ticks.here(3, pairs, steps - 1)

        @pl.when(step == pairs + 1)
        def _():
            recv_all(first)
            mine = vec[:, part(spot.z)]
            for i in range(depth - 1):
                mine = mine + vec_z[i]
            vec_g[spot.g] = mine
            start_all(second)

        @pl.when(step == steps - 1)
        def _():
            recv_all(second)
            whole = vec_g[0]
            for i in range(1, groups):
                whole = whole + vec_g[i]
            vec_out[...] = whole
            send_done(first)
            send_done(second)
            keep.wait()
            swap.finish()

    at = lambda s: jnp.minimum(s, pairs - 1)
    whole = lambda *dims: pl.BlockSpec(dims, lambda s: (0,) * len(dims))
    column = lambda rows: pl.BlockSpec((rows, LANES), lambda s: (0, at(s)))
    return pl.pallas_call(
        kernel,
        grid=(steps,),
        in_specs=[
            pl.BlockSpec((5, span, LANES), lambda s: (0, 0, at(s))),
            column(few), still(*marks.shape), still(*place.shape), column(span), column(span),
            pl.BlockSpec((1, 8, span), lambda s: (at(s), 0, 0)),
            pl.BlockSpec((1, 8, LANES), lambda s: (at(s), 0, 0)),
        ]
        + [ANYSPEC] * (given + 1)
        + [
            pl.BlockSpec(
                (1, columns, columns), lambda s: (jnp.clip(s - pairs, 0, count - 1), 0, 0), pipeline_mode=pl.Buffered(1)
            ),
            still(span, columns), ANYSPEC, still(*hidden_sums.shape), still(*feed_sums.shape), still(*norm_sums.shape),
        ],
        out_specs=[whole(v.shape[0], block, width) for v in views]
        + [whole(count, block, width), whole(vec_rows, width), ANYSPEC, ANYSPEC],
        out_shape=[jax.ShapeDtypeStruct((v.shape[0], block, width), F32) for v in views]
        + [
            jax.ShapeDtypeStruct((count, block, width), F32),
            jax.ShapeDtypeStruct((vec_rows, width), F32),
            jax.ShapeDtypeStruct((span, columns), BF),
            jax.ShapeDtypeStruct(parts.shape, BF),
        ],
        scratch_shapes=[
            pltpu.VMEM((span, span), F32),
            pltpu.VMEM((5, span, columns), BF),
            pltpu.VMEM((few, columns), BF),
            pltpu.VMEM((8, columns), F32),
            pltpu.VMEM((span, LANES), F32),
            pltpu.VMEM((span, LANES), F32),
            pltpu.VMEM((span, columns), F32),
            pltpu.VMEM((vec_rows, columns), F32),
            pltpu.VMEM((depth - 1, vec_rows, width), F32),
            pltpu.VMEM((groups, vec_rows, width), F32),
            dma(total),
            dma(total),
            dma(early + 3),
            pltpu.SemaphoreType.REGULAR,
        ]
        + [box for some in boxes for box in some],
        compiler_params=kernel_params(3),
        name="attend_back_and_reduce",
    )(projected, query_global, marks, place, attended, attended_adjoint, log_sums, log_sums_global, *views, parts, full_in,
      sequence, mixture_adjoint, hidden_sums, feed_sums, norm_sums)


def up_parts(matrix, ratio, parts):
    rows, columns = matrix.shape
    r = columns // (ratio * parts)
    return matrix.reshape(rows, ratio, parts, r).transpose(2, 0, 1, 3).reshape(parts, rows, ratio * r)


def up_whole(stack, ratio):
    parts, rows, columns = stack.shape
    r = columns // ratio
    return stack.reshape(parts, rows, ratio, r).transpose(1, 2, 0, 3).reshape(rows, parts * columns)


def per_device(mesh, tokens, out_cotangent, lengths, places, deal, in_weights, out_weight, up_weight, down_weight, vectors,
               first_in, first_out, first_up, first_down, first_vectors,
               second_in, second_out, second_up, second_down, second_vectors):
    groups, depth = mesh.shape["grp"], mesh.shape["dp"]
    ratio = groups // depth
    devices = groups * depth
    span = tokens.shape[1]
    quarters = FF // D
    ids = jnp.arange(devices, dtype=jnp.int32)
    inverse = jnp.sum(jnp.where(deal[None, :] == ids[:, None], ids[None, :], 0), axis=1)
    sequence = tokens[0]
    order = np.array([1, 2, 0, 4, 5, 3])

    low_in = jnp.stack([in_weights[i] for i in order]).astype(BF)
    low_rest = jnp.concatenate([out_weight.astype(BF)[None], up_parts(up_weight.astype(BF), ratio, quarters)])
    low_down = down_weight.astype(BF).reshape(quarters, -1, down_weight.shape[1])
    nv = vectors.shape[0]
    low_vectors = jnp.pad(vectors, ((0, 16 - nv), (0, 0))).astype(BF)

    shape_parts = (devices, span // devices, D)

    (full_in, full_out, full_up, _, projected, query_global, attended, log_sums, log_sums_global,
     cotangent_parts, marks, place, vector_rows) = project_and_attend(
        mesh, low_in, low_rest, low_vectors, sequence, places, lengths[:, None], out_cotangent.reshape(shape_parts)
    )
    hidden_bias = vector_rows[5 : 5 + quarters].reshape(groups, quarters, -1).transpose(1, 0, 2).reshape(quarters, D)
    cotangent_parts = cotangent_parts.at[deal].get(mode="promise_in_bounds")
    full_down, hidden, slope, first_low, normal_one, spread_one, layer_out, feed_low, sum_adjoint, feed_sums = feed_forward(
        mesh, sequence, attended, full_out, full_up, low_down, cotangent_parts, vector_rows, hidden_bias, marks
    )
    up_change, hidden_sums, mixture_adjoint, part_down, layer_parts, out_change, attended_adjoint, norm_sums = feed_backward(
        mesh, feed_low, first_low, hidden, slope, full_up, full_down, sum_adjoint, attended, full_out, normal_one, spread_one,
        vector_rows, layer_out.reshape(shape_parts)
    )
    layer_parts = layer_parts.at[inverse].get(mode="promise_in_bounds")
    hidden_bias_change = hidden_sums[:, 0].reshape(quarters, groups, -1).transpose(1, 0, 2).reshape(quarters, D)
    part_up, part_out, part_in, part_vectors, token_gradient, layer_mine = attend_back_and_reduce(
        mesh, projected, query_global, marks, place, attended, attended_adjoint, log_sums, log_sums_global,
        (up_change, out_change), layer_parts, full_in, sequence, mixture_adjoint, hidden_bias_change, feed_sums, norm_sums,
        order
    )

    step_count = jnp.float32(STEP)
    fix_first = 1.0 - jnp.power(jnp.float32(BETA_FIRST), step_count)
    fix_second = 1.0 - jnp.power(jnp.float32(BETA_SECOND), step_count)

    def adam(weight, gradient, moment, square, decay):
        return adam_update(weight, gradient, moment, square, decay, fix_first, fix_second)

    part_up = up_whole(part_up, ratio)
    part_out = part_out[0]
    part_down = part_down.reshape(down_weight.shape)
    update_in, moment_in, square_in = adam(in_weights, part_in, first_in, second_in, WEIGHT_DECAY)
    update_out, moment_out, square_out = adam(out_weight, part_out, first_out, second_out, WEIGHT_DECAY)
    update_up, moment_up, square_up = adam(up_weight, part_up, first_up, second_up, WEIGHT_DECAY)
    update_down, moment_down, square_down = adam(down_weight, part_down, first_down, second_down, WEIGHT_DECAY)
    update_vectors, moment_vectors, square_vectors = adam(vectors, part_vectors[:nv], first_vectors, second_vectors, 0.0)
    return (
        layer_mine.reshape(tokens.shape), token_gradient[None],
        update_in, update_out, update_up, update_down, update_vectors,
        moment_in, moment_out, moment_up, moment_down, moment_vectors,
        square_in, square_out, square_up, square_down, square_vectors,
    )


def solution(mesh):
    sequences = P(("grp", "dp"), None, None)
    stack, matrix, rows = P(None, "grp", "dp"), P("grp", "dp"), P(None, "dp")
    packed = (stack, matrix, matrix, matrix, rows)
    return jax.shard_map(
        lambda *arrays: per_device(mesh, *arrays),
        mesh=mesh,
        in_specs=(sequences, sequences, P(), P(), P()) + packed * 3,
        out_specs=(sequences, sequences) + packed * 3,
        check_vma=False,
    )
```

```python
import jax
import jax.numpy as jnp
import numpy as np
from jax import lax
from jax.experimental import pallas as pl
from jax.experimental.pallas import tpu as pltpu
from jax.sharding import PartitionSpec as P

D = 1024
H = 16
HD = 64
FF = 4096
W = 512
NG = 64
STEP = 10

EPS_NORM = 1e-05
WEIGHT_DECAY = 0.1
BETA_FIRST = 0.5
BETA_SECOND = 0.999
EPS_ADAM = 1e-08
NEGATIVE = -1e30

MESH = pl.DeviceIdType.MESH
MIB = 1 << 20
BF = jnp.bfloat16
F32 = jnp.float32
LANES = 128
ROWS = 256
ANYSPEC = pl.BlockSpec(memory_space=pl.ANY)
SMEMSPEC = pl.BlockSpec(memory_space=pltpu.SMEM)


def product(left_side, right_side):
    return jnp.dot(left_side, right_side, preferred_element_type=F32)


def product_back(left_side, right_side):
    return lax.dot_general(
        left_side, right_side, (((1,), (1,)), ((), ())), preferred_element_type=F32
    )


def product_left(left_side, right_side):
    return lax.dot_general(
        left_side, right_side, (((0,), (0,)), ((), ())), preferred_element_type=F32
    )


def column_sums(matrix):
    return jnp.sum(matrix.astype(F32), axis=0)


def adam_update(weight, gradient, moment, square, decay_rate, fix_first, fix_second):
    moment_new = BETA_FIRST * moment + (1.0 - BETA_FIRST) * gradient
    square_new = BETA_SECOND * square + (1.0 - BETA_SECOND) * gradient * gradient
    update = moment_new / fix_first / (jnp.sqrt(square_new / fix_second) + EPS_ADAM)
    return (update + decay_rate * weight, moment_new, square_new)


class Spot:
    def __init__(self, groups, depth):
        self.nb = groups // 4
        self.nz = depth
        self.groups = groups
        g = lax.axis_index("grp")
        self.g = g
        self.z = lax.axis_index("dp")
        self.c = lax.rem(g, 2)
        self.b = lax.rem(lax.div(g, 2), self.nb)
        self.a = lax.div(g, 2 * self.nb)

    def at(self, a=None, b=None, c=None, z=None):
        a = self.a if a is None else a
        b = self.b if b is None else b
        c = self.c if c is None else c
        z = self.z if z is None else z
        return ((a * self.nb + b) * 2 + c, z)

    def b_off(self, i):
        return lax.rem(self.b + i, self.nb)

    def z_off(self, i):
        return lax.rem(self.z + i, self.nz)

    def z_flip(self, bit):
        return self.z + bit - 2 * bit * lax.rem(lax.div(self.z, bit), 2)

    def z_mask(self, mask):
        out = self.z
        bit = 1
        while bit < self.nz:
            if mask & bit:
                out = out + bit - 2 * bit * lax.rem(lax.div(self.z, bit), 2)
            bit *= 2
        return out

    def neighbours(self):
        out = [self.at(a=1 - self.a), self.at(c=1 - self.c)]
        out += [self.at(b=self.b_off(i)) for i in range(1, self.nb)]
        out += [self.at(z=self.z_off(i)) for i in range(1, self.nz)]
        return out


def greet(targets):
    barrier = pltpu.get_barrier_semaphore()
    for target in targets:
        pl.semaphore_signal(barrier, inc=1, device_id=target, device_id_type=MESH)
    pl.semaphore_wait(barrier, len(targets))


class Sems:
    def __init__(self, send, recv):
        self.send, self.recv, self.used = send, recv, 0

    def copy(self, src, dst, target):
        i = self.used
        self.used += 1
        return pltpu.make_async_remote_copy(
            src_ref=src,
            dst_ref=dst,
            send_sem=self.send.at[i],
            recv_sem=self.recv.at[i],
            device_id=target,
            device_id_type=MESH,
        )


def start_all(copies):
    for copy in copies:
        copy.start()


def recv_all(copies):
    for copy in copies:
        copy.wait_recv()


def send_done(copies):
    for copy in copies:
        copy.wait_send()


def add_all(terms):
    if len(terms) == 2:
        return terms[0] + terms[1]
    return sum(t.astype(F32) for t in terms).astype(terms[0].dtype)


def gather_copies(nb, nz):
    return (nz - 1) + 1 + (nb - 1) + (nb - 1) + 1 + 1


class GatherPiece:
    def __init__(self, spot, sems, local_sem, src, out):
        a, b, c, z = spot.a, spot.b, spot.c, spot.z
        rows, width = src.shape
        half = rows // 2
        own = pl.ds(pl.multiple_of(z * width, LANES), width)
        top, low = pl.ds(0, half), pl.ds(half, half)
        mine = out.at[a, b, c, :, own]
        self.local = pltpu.make_async_copy(src, mine, local_sem)
        self.phases = [[sems.copy(src, mine, spot.at(z=spot.z_off(i))) for i in range(1, spot.nz)]]
        self.along = len(self.phases)
        self.phases += [
            [sems.copy(out.at[a, b, c, top], out.at[a, b, c, top], spot.at(a=1 - a))]
            + [
                sems.copy(out.at[a, b, c, low], out.at[a, b, c, low], spot.at(b=spot.b_off(i)))
                for i in range(1, spot.nb)
            ],
            [
                sems.copy(out.at[:, b, c, top], out.at[:, b, c, top], spot.at(b=spot.b_off(i)))
                for i in range(1, spot.nb)
            ]
            + [sems.copy(out.at[a, :, c, low], out.at[a, :, c, low], spot.at(a=1 - a))],
            [sems.copy(out.at[:, :, c], out.at[:, :, c], spot.at(c=1 - c))],
        ]

    def start(self, p):
        if p == 0:
            self.local.start()
        if p == self.along:
            self.local.wait()
        start_all(self.phases[p])

    def arrive(self, p):
        recv_all(self.phases[p])

    def close(self):
        for phase in self.phases:
            send_done(phase)


class Swap:
    def __init__(self, spot, sems, local_sem, src, dst):
        devices = spot.groups * spot.nz
        me = spot.g * spot.nz + spot.z
        self.local = pltpu.make_async_copy(src.at[me], dst.at[me], local_sem)
        self.copies = []
        for i in range(1, devices):
            other = lax.rem(me + i, devices)
            self.copies.append(
                sems.copy(src.at[other], dst.at[me], (lax.div(other, spot.nz), lax.rem(other, spot.nz)))
            )

    def start(self, part, parts):
        if part == 0:
            self.local.start()
        n = len(self.copies)
        start_all(self.copies[part * n // parts : (part + 1) * n // parts])

    def finish(self):
        self.local.wait()
        recv_all(self.copies)
        send_done(self.copies)


def reorder(index_ref, source, target):
    def one(i, carry):
        target[i] = source[index_ref[i]]
        return carry

    lax.fori_loop(0, target.shape[0], one, 0)


def timeline(pieces, times):
    phases = len(pieces[0].phases)
    steps = {}
    for t in reversed(range(len(pieces))):
        for p in range(phases + 1):
            steps.setdefault(times[t][p], []).append((t, p))

    def run(events):
        for t, p in events:
            if p > 0:
                pieces[t].arrive(p - 1)
            if p < phases:
                pieces[t].start(p)
            else:
                pieces[t].close()

    return {s: (lambda events=events: run(events)) for s, events in steps.items()}


class Ticks:
    def __init__(self, per):
        self.per, self.actions = per, {}

    def add(self, tick, action):
        self.actions.setdefault(tick, []).append(action)

    def add_all(self, actions):
        for tick, action in actions.items():
            self.add(tick, action)

    def here(self, c, first, last):
        for tick in sorted(self.actions):
            if tick % self.per == c and first <= tick // self.per <= last:

                @pl.when(pl.program_id(0) == tick // self.per)
                def _(mine=self.actions[tick]):
                    for action in mine:
                        action()


def during(first, last):
    return pl.when(jnp.logical_and(pl.program_id(0) >= first, pl.program_id(0) <= last))


def in_chunks(span, body):
    def step(i, carry):
        body(pl.ds(pl.multiple_of(i * ROWS, ROWS), ROWS))
        return carry

    lax.fori_loop(0, span // ROWS, step, 0)


def reduce_copies(nb, nz):
    return 1 + (nb - 1) + 1 + 1 + (nb - 1) + (nz - 1)


class ReducePiece:
    def __init__(self, spot, sems, local_sem, src, width, boxes, finish):
        self.spot, self.finish, self.width = spot, finish, width
        tile, self.r0, self.r1b, self.r1a, self.r2a, self.r2b, self.r3 = boxes
        a, b, c, z = spot.a, spot.b, spot.c, spot.z
        self.acc = acc = tile.at[:, :, c] if src is None else tile.at[:, :, 0]
        other = (tile if src is None else src).at[:, :, 1 - c]
        half = tile.shape[-2] // 2
        self.half = half
        top, low = pl.ds(0, half), pl.ds(half, half)
        self.local = None if src is None else pltpu.make_async_copy(src.at[:, :, c], acc, local_sem)
        columns = lambda zz: pl.ds(pl.multiple_of(zz * self.width, LANES), self.width)
        self.phases = [
            [sems.copy(other, self.r0, spot.at(c=1 - c))],
            [
                sems.copy(acc.at[:, spot.b_off(i), top], self.r1b.at[i - 1], spot.at(b=spot.b_off(i)))
                for i in range(1, spot.nb)
            ]
            + [sems.copy(acc.at[1 - a, :, low], self.r1a, spot.at(a=1 - a))],
            [sems.copy(acc.at[1 - a, b, top], self.r2a, spot.at(a=1 - a))]
            + [
                sems.copy(acc.at[a, spot.b_off(i), low], self.r2b.at[i - 1], spot.at(b=spot.b_off(i)))
                for i in range(1, spot.nb)
            ],
        ]
        self.columns = columns
        self.landed = []
        bit, slot = 1, 0
        while bit < spot.nz:
            masks = [m for m in range(spot.nz) if m & bit and m % bit == 0]
            target = spot.at(z=spot.z_flip(bit))
            self.phases.append(
                [
                    sems.copy(acc.at[a, b, :, columns(spot.z_mask(m))], self.r3.at[slot + i], target)
                    for i, m in enumerate(masks)
                ]
            )
            self.landed.append([(m ^ bit, slot + i) for i, m in enumerate(masks)])
            slot += len(masks)
            bit *= 2

    def start(self, p):
        if p == 0 and self.local is not None:
            self.local.start()
        start_all(self.phases[p])

    def arrive(self, p):
        spot, acc = self.spot, self.acc
        a, b = spot.a, spot.b
        top, low = pl.ds(0, self.half), pl.ds(self.half, self.half)
        recv_all(self.phases[p])
        if p == 0:
            if self.local is not None:
                self.local.wait()
            for i in range(2):
                for j in range(spot.nb):
                    acc[i, j] = acc[i, j] + self.r0[i, j]
        if p == 1:
            for i in range(2):
                acc[i, b, top] = add_all([acc[i, b, top]] + [self.r1b[k, i] for k in range(spot.nb - 1)])
            for j in range(spot.nb):
                acc[a, j, low] = acc[a, j, low] + self.r1a[j]
        if p == 2:
            acc[a, b, top] = acc[a, b, top] + self.r2a[...]
            acc[a, b, low] = add_all([acc[a, b, low]] + [self.r2b[k] for k in range(spot.nb - 1)])
        if p >= 3:
            for mask, slot in self.landed[p - 3]:
                block = self.columns(spot.z_mask(mask))
                if p == len(self.phases) - 1:
                    self.finish(acc[a, b, :, block].astype(F32) + self.r3[slot].astype(F32))
                else:
                    acc[a, b, :, block] = acc[a, b, :, block] + self.r3[slot]

    def close(self):
        for phase in self.phases:
            send_done(phase)


def reduce_boxes(nb, nz, rows, columns):
    half = rows // 2
    return [
        pltpu.VMEM((2, nb, 2, rows, columns), BF),
        pltpu.VMEM((2, nb, rows, columns), BF),
        pltpu.VMEM((nb - 1, 2, half, columns), BF),
        pltpu.VMEM((nb, half, columns), BF),
        pltpu.VMEM((half, columns), BF),
        pltpu.VMEM((nb - 1, half, columns), BF),
        pltpu.VMEM((nz - 1, rows, columns // nz), BF),
    ]


def key_parts(span, block):
    low = max(0, (block - 1) * ROWS)
    high = min(span, (block + 2) * ROWS)
    if low <= ROWS:
        return [(0, high)]
    return [(0, ROWS), (low, high)]


def head_masks():
    lane = lax.broadcasted_iota(jnp.int32, (1, LANES), 1)
    return (lane < HD, lane >= HD)


def only(mask, block):
    return jnp.where(mask, block, jnp.zeros_like(block))


def make_bias(marks_ref, bias):
    span = bias.shape[0]
    for i in range(0, span, ROWS):
        part = slice(i, i + ROWS)
        distance = lax.broadcasted_iota(jnp.int32, (ROWS, span), 0) + i - lax.broadcasted_iota(jnp.int32, (ROWS, span), 1)
        near = jnp.where(jnp.abs(distance) <= W // 2, 0.0, NEGATIVE)
        near = jnp.where(marks_ref[part, 1:2] > 0.5, 0.0, near)
        bias[part, :] = jnp.where(marks_ref[part, 0:1] > 0.5, near, NEGATIVE)


def attend_local(refs, bias_ref, a_ref, lse_ref, tick):
    k_ref, v_ref, q_ref = refs
    span = q_ref.shape[0]
    masks = head_masks()
    query = q_ref[...] * jnp.asarray(HD ** (-0.5), BF)
    values_flip = v_ref[...].T
    for block in range(span // ROWS):
        tick(block)
        rows = slice(block * ROWS, (block + 1) * ROWS)
        parts = key_parts(span, block)
        flips = []
        for h in range(2):
            head_query = only(masks[h], query[rows])
            scored = [
                product_back(k_ref[lo:hi, :], head_query) + bias_ref[lo:hi, rows] for lo, hi in parts
            ]
            top = jnp.max(scored[0], axis=0, keepdims=True)
            for s in scored[1:]:
                top = jnp.maximum(top, jnp.max(s, axis=0, keepdims=True))
            weights = [jnp.exp(s - top) for s in scored]
            total = sum(jnp.sum(w, axis=0, keepdims=True) for w in weights)
            lse_ref[0, h : h + 1, rows] = top + jnp.log(total)
            mixed = sum(
                product(values_flip[h * HD : (h + 1) * HD, lo:hi], w.astype(BF))
                for (lo, hi), w in zip(parts, weights)
            )
            flips.append(mixed * (1.0 / total))
        a_ref[rows, :] = jnp.concatenate(flips, axis=0).T.astype(BF)


def attend_global(refs, qg_ref, marks_ref, place_ref, a_ref, lse_global_ref):
    kg_ref, vg_ref = refs
    masks = head_masks()
    query = qg_ref[...] * jnp.asarray(HD ** (-0.5), BF)
    stacked = jnp.concatenate([only(m, query) for m in masks], axis=0)
    scores = product_back(kg_ref[...], stacked) + jnp.where(marks_ref[:, 0:1] > 0.5, 0.0, NEGATIVE)
    top = jnp.max(scores, axis=0, keepdims=True)
    probs = jnp.exp(scores - top)
    total = jnp.sum(probs, axis=0, keepdims=True)
    lse_global_ref[...] = jnp.broadcast_to(top + jnp.log(total), (8, LANES))
    probs = (probs * (1.0 / total)).astype(BF)
    mixed = product_left(probs, vg_ref[...])
    global_out = jnp.where(masks[0], mixed[:NG], mixed[NG:]).astype(BF)
    global_rows = product(place_ref[...], global_out)
    is_global = marks_ref[:ROWS, 1:2] > 0.5
    a_ref[:ROWS, :] = jnp.where(is_global, global_rows, a_ref[:ROWS, :].astype(F32)).astype(BF)


def attention_backward(refs, qg_ref, bias_ref, marks_ref, place_ref, a_ref, da_ref, lse_ref, lse_global_ref,
                       back_refs, dqg_ref, sums_ref, dk_sum, dv_sum, tick):
    k_ref, v_ref, q_ref, kg_ref, vg_ref = refs
    dk_ref, dv_ref, dq_ref, dkg_ref, dvg_ref = back_refs
    span = q_ref.shape[0]
    masks = head_masks()
    scale = HD ** (-0.5)
    query = q_ref[...] * jnp.asarray(scale, BF)
    keys_flip = k_ref[...].T
    query_global = qg_ref[...] * jnp.asarray(scale, BF)
    stacked = jnp.concatenate([only(m, query_global) for m in masks], axis=0)
    adjoint_global = product_left(place_ref[...], da_ref[:ROWS, :]).astype(BF)
    adjoint_stacked = jnp.concatenate([only(m, adjoint_global) for m in masks], axis=0)
    scores = product_back(kg_ref[...], stacked) + jnp.where(marks_ref[:, 0:1] > 0.5, 0.0, NEGATIVE)
    probs = jnp.exp(scores - lse_global_ref[0, 0:1, :])
    prob_adjoint = product_back(vg_ref[...], adjoint_stacked)
    center = jnp.sum(probs * prob_adjoint, axis=0, keepdims=True)
    score_adjoint = (probs * (prob_adjoint - center)).astype(BF)
    mixed = product_left(score_adjoint, kg_ref[...]) * scale
    dqg_ref[...] = jnp.where(masks[0], mixed[:NG], mixed[NG:]).astype(BF)
    dkg_ref[...] = product(score_adjoint, stacked).astype(BF)
    dvg_ref[...] = product(probs.astype(BF), adjoint_stacked).astype(BF)
    first = jnp.where(marks_ref[:ROWS, 1:2] > 0.5, 0.0, da_ref[:ROWS, :].astype(F32)).astype(BF)
    adjoint = jnp.concatenate([first, da_ref[ROWS:, :]], axis=0)
    inner = adjoint.astype(F32) * a_ref[...].astype(F32)
    picker = (lax.broadcasted_iota(jnp.int32, (8, LANES), 0) == lax.div(lax.broadcasted_iota(jnp.int32, (8, LANES), 1), HD)).astype(F32)
    centers = lax.dot_general(
        picker, inner, (((1,), (1,)), ((), ())), preferred_element_type=F32, precision=lax.Precision.HIGHEST
    )
    dk_sum[...] = jnp.zeros_like(dk_sum)
    dv_sum[...] = jnp.zeros_like(dv_sum)
    for block in range(span // ROWS):
        tick(block)
        rows = slice(block * ROWS, (block + 1) * ROWS)
        parts = key_parts(span, block)
        flips = []
        for h in range(2):
            head_query = only(masks[h], query[rows])
            head_adjoint = only(masks[h], adjoint[rows])
            log_sum = lse_ref[0, h : h + 1, rows]
            center = centers[h : h + 1, rows]
            mixed = None
            for lo, hi in parts:
                s = product_back(k_ref[lo:hi, :], head_query) + bias_ref[lo:hi, rows]
                weights = jnp.exp(s - log_sum)
                prob_adjoint = product_back(v_ref[lo:hi, :], head_adjoint)
                score_adjoint = (weights * (prob_adjoint - center)).astype(BF)
                dv_sum[lo:hi, :] += product(weights.astype(BF), head_adjoint)
                dk_sum[lo:hi, :] += product(score_adjoint, head_query)
                part = product(keys_flip[h * HD : (h + 1) * HD, lo:hi], score_adjoint)
                mixed = part if mixed is None else mixed + part
            flips.append(mixed)
        dq_ref[rows, :] = (jnp.concatenate(flips, axis=0).T * scale).astype(BF)
    dk_ref[...] = dk_sum[...].astype(BF)
    dv_ref[...] = dv_sum[...].astype(BF)
    sums = [jnp.sum(r[...].astype(F32), axis=0, keepdims=True) for r in (dq_ref, dv_ref, dqg_ref, dvg_ref)]
    sums_ref[...] = jnp.concatenate(sums + [jnp.zeros((4, LANES), F32)], axis=0)


def gelu_and_slope(u):
    e = jnp.exp2(u * (u * (-0.5 * 1.4426950408889634)))
    t = 1.0 / (1.0 + (0.3275911 * 0.7071067811865476) * jnp.abs(u))
    tail = 0.5 * -1.453152027 + t * (0.5 * 1.061405429)
    tail = 0.5 * -0.284496736 + t * (0.5 * 1.421413741 + t * tail)
    tail = t * (0.5 * 0.254829592 + t * tail) * e
    phi = jnp.where(u >= 0.0, 1.0 - tail, tail)
    return u * phi, phi + u * e * 0.3989422804014327


def normalize(mixture):
    centered = mixture - jnp.mean(mixture, axis=-1, keepdims=True)
    spread = lax.rsqrt(jnp.mean(centered * centered, axis=-1, keepdims=True) + EPS_NORM)
    return centered * spread, spread


def normalize_back(adjoint, normal, spread, gain):
    scaled = adjoint * gain
    mean = jnp.mean(scaled, axis=-1, keepdims=True)
    along = jnp.mean(scaled * normal, axis=-1, keepdims=True)
    return spread * (scaled - mean - normal * along)


def kernel_params(collective=None, **more):
    if collective is not None:
        more.update(collective_id=collective, has_side_effects=True)
    return pltpu.CompilerParams(vmem_limit_bytes=61 * MIB, **more)


def dma(count):
    return pltpu.SemaphoreType.DMA((count,))


def still(*shape):
    return pl.BlockSpec(shape, lambda s: (0,) * len(shape), pipeline_mode=pl.Buffered(1))


def full_shape(nb, block, columns, *lead):
    return lead + (2, nb, 2, block, columns)


def everyone(spot):
    devices = spot.groups * spot.nz
    me = spot.g * spot.nz + spot.z
    ids = [lax.rem(me + i, devices) for i in range(1, devices)]
    return [(lax.div(i, spot.nz), lax.rem(i, spot.nz)) for i in ids]


def project_and_attend(mesh, low_in, low_rest, low_vectors, sequence, places, lengths, parts):
    groups, depth = mesh.shape["grp"], mesh.shape["dp"]
    nb = groups // 4
    count, block, width = low_in.shape
    rest = low_rest.shape[0]
    span, columns = sequence.shape
    devices = groups * depth
    few = places.shape[1]
    pairs = H // 2
    total = (count + rest) * gather_copies(nb, depth) + depth - 1 + devices - 1
    lag = 3
    local_count = 3
    attend = lag + local_count
    project = attend + pairs
    glob = project + count - local_count
    together = 2
    steps = glob + pairs // together

    def slot(s):
        return 4 * s if s < attend else 4 * attend + 6 * (s - attend)

    def kernel(in_ref, rest_ref, vec_ref, seq_ref, places_ref, lengths_ref, part_ref,
               full_ref, out_ref, up_ref, vec_full_ref, proj_ref, few_ref, a_ref, lse_ref, lse_global_ref, swapped_ref,
               marks_ref, place_ref, vec_out_ref,
               weight, vec, proj, bias, send, recv, local):
        spot = Spot(groups, depth)
        sems = Sems(send, recv)
        pairs_of = [(in_ref.at[t], full_ref.at[t]) for t in range(count)]
        pairs_of += [(rest_ref.at[0], out_ref)] + [(rest_ref.at[1 + q], up_ref.at[q]) for q in range(rest - 1)]
        pieces = [GatherPiece(spot, sems, local.at[t], src, out) for t, (src, out) in enumerate(pairs_of)]
        swap = Swap(spot, sems, local.at[count + rest], part_ref, swapped_ref)
        own = pl.ds(pl.multiple_of(spot.z * width, LANES), width)
        mine = vec_full_ref.at[:, own]
        vec_local = pltpu.make_async_copy(vec_ref, mine, local.at[count + rest + 1])
        vec_sends = [sems.copy(vec_ref, mine, spot.at(z=spot.z_off(i))) for i in range(1, depth)]
        keep = [
            pltpu.make_async_copy(proj.at[t], proj_ref.at[t], local.at[count + rest + 2 + t]) for t in range(count - 1)
        ]
        step = pl.program_id(0)
        ticks = Ticks(4)
        times = []
        for t in range(count + rest):
            if t < local_count:
                times.append([max(0, slot(t - 1) + 1), slot(t), slot(t + 1) + 1, slot(t + 2) + 2, slot(t + 3) + 3])
            else:
                times.append([slot(t - 2) + 1, slot(t), slot(t + 2) + 1, slot(t + 4) + 2, slot(t + 5) + 3])
        ticks.add_all(timeline(pieces, times))
        for j in range(8):
            ticks.add(4 * (attend + 2 * j if j < 4 else project + j - 4) + 2, lambda j=j: swap.start(j, 8))

        @pl.when(step == 0)
        def _():
            greet(everyone(spot))
            vec_local.start()
            start_all(vec_sends)

        for c in range(4):
            ticks.here(c, 0, attend - 1)

        @pl.when(step == 0)
        def _():
            me = spot.g * depth + spot.z
            spots = places_ref[pl.ds(me, 1), :]
            length = lengths_ref[pl.ds(me, 1), :]
            for i in range(0, span, ROWS):
                hit = (lax.broadcasted_iota(jnp.int32, (ROWS, few), 0) + i == spots).astype(F32)
                if i == 0:
                    place_ref[...] = hit.astype(BF)
                is_global = jnp.max(hit, axis=1, keepdims=True)
                lane = lax.broadcasted_iota(jnp.int32, (ROWS, LANES), 1)
                valid = (lax.broadcasted_iota(jnp.int32, (ROWS, LANES), 0) + i < length).astype(F32)
                marks_ref[i : i + ROWS, :] = jnp.where(lane == 0, valid, jnp.where(lane == 1, is_global, 0.0))
            make_bias(marks_ref, bias)

        @pl.when(step == lag)
        def _():
            vec_local.wait()
            recv_all(vec_sends)
            send_done(vec_sends)
            pltpu.sync_copy(vec_full_ref, vec)
            vec_out_ref[...] = vec[...].astype(F32)

        def offset(row):
            index = lax.broadcasted_iota(jnp.int32, vec.shape, 0)
            return jnp.sum(jnp.where(index == row, vec[...].astype(F32), 0.0), axis=0, keepdims=True)

        for c in range(4):
            ticks.here(c, project, steps - 1)

        def project_one(t):
            pltpu.sync_copy(full_ref.at[t], weight)
            added = offset(jnp.where(t == 1, 1, jnp.where(t == 2, 0, jnp.where(t == 4, 4, 15))))

            def body(rows):
                matrix = weight[...].reshape(groups * block, columns)
                proj[t, rows, :] = (product(seq_ref[rows, :], matrix) + added).astype(BF)

            in_chunks(span, body)

        first_part = jnp.logical_and(step >= lag, step < attend)
        second_part = jnp.logical_and(step >= project, step < glob - 1)
        pl.when(jnp.logical_or(first_part, second_part))(
            lambda: project_one(jnp.where(step < attend, step - lag, step - project + local_count))
        )
        for t in range(count - 1):
            pl.when(step == (lag + t if t < local_count else project + t - local_count))(keep[t].start)

        @pl.when(step == glob - 1)
        def _():
            pltpu.sync_copy(full_ref.at[count - 1], weight)
            matrix = weight[...].reshape(groups * block, columns)
            rows = product_left(place_ref[...], seq_ref[:ROWS, :]).astype(BF)
            few_ref[...] = (product(rows, matrix) + offset(3)).astype(BF)

        @during(attend, project - 1)
        def _():
            lanes = pl.ds(pl.multiple_of((step - attend) * LANES, LANES), LANES)
            attend_local(
                [proj.at[i, :, lanes] for i in range(local_count)], bias, a_ref.at[:, lanes], lse_ref,
                lambda c: ticks.here(c, attend, project - 1),
            )

        @pl.when(step >= glob)
        def _():
            def one(i, carry):
                pair = (step - glob) * together + i
                lanes = pl.ds(pl.multiple_of(pair * LANES, LANES), LANES)
                attend_global(
                    [proj.at[i, :, lanes] for i in range(local_count, count - 1)], few_ref.at[:, lanes], marks_ref, place_ref,
                    a_ref.at[:, lanes], lse_global_ref.at[pair],
                )
                return carry

            lax.fori_loop(0, together, one, 0)

        @pl.when(step == steps - 1)
        def _():
            for copy in keep:
                copy.wait()
            swap.finish()

    at = lambda s: jnp.clip(s - attend, 0, pairs - 1)
    results = pl.pallas_call(
        kernel,
        grid=(steps,),
        in_specs=[ANYSPEC] * 3 + [still(span, columns), still(*places.shape), still(*lengths.shape), ANYSPEC],
        out_specs=[ANYSPEC] * 5
        + [
            pl.BlockSpec((few, columns), lambda s: (0, 0)),
            pl.BlockSpec((span, columns), lambda s: (0, 0)),
            pl.BlockSpec((1, 8, span), lambda s: (at(s), 0, 0)),
            pl.BlockSpec((pairs, 8, LANES), lambda s: (0, 0, 0)),
            ANYSPEC,
            pl.BlockSpec((span, LANES), lambda s: (0, 0)),
            pl.BlockSpec((ROWS, few), lambda s: (0, 0)),
            pl.BlockSpec((low_vectors.shape[0], columns), lambda s: (0, 0)),
        ],
        out_shape=[
            jax.ShapeDtypeStruct(full_shape(nb, block, columns, count), BF),
            jax.ShapeDtypeStruct(full_shape(nb, block, columns), BF),
            jax.ShapeDtypeStruct(full_shape(nb, block, columns, rest - 1), BF),
            jax.ShapeDtypeStruct((low_vectors.shape[0], columns), BF),
            jax.ShapeDtypeStruct((count - 1, span, columns), BF),
            jax.ShapeDtypeStruct((few, columns), BF),
            jax.ShapeDtypeStruct((span, columns), BF),
            jax.ShapeDtypeStruct((pairs, 8, span), F32),
            jax.ShapeDtypeStruct((pairs, 8, LANES), F32),
            jax.ShapeDtypeStruct(parts.shape, BF),
            jax.ShapeDtypeStruct((span, LANES), F32),
            jax.ShapeDtypeStruct((ROWS, few), BF),
            jax.ShapeDtypeStruct((low_vectors.shape[0], columns), F32),
        ],
        scratch_shapes=[
            pltpu.VMEM(full_shape(nb, block, columns), BF),
            pltpu.VMEM((low_vectors.shape[0], columns), BF),
            pltpu.VMEM((count - 1, span, columns), BF),
            pltpu.VMEM((span, span), F32),
            dma(total),
            dma(total),
            dma(count + rest + 2 + count - 1),
        ],
        compiler_params=kernel_params(0),
        name="project_and_attend",
    )(low_in, low_rest, low_vectors, sequence, places, lengths, parts)
    square = (groups * block, columns)
    full_in, full_out, full_up = results[:3]
    return (full_in.reshape((count,) + square), full_out.reshape(square), full_up.reshape((rest - 1,) + square)) + tuple(
        results[3:]
    )


def feed_forward(mesh, sequence, attended, full_out, full_up, shards, parts, index, vectors, hidden_bias, valid):
    groups, depth = mesh.shape["grp"], mesh.shape["dp"]
    nb = groups // 4
    span, columns = sequence.shape
    count, block, width = shards.shape
    devices = groups * depth
    total = count * gather_copies(nb, depth) + devices - 1
    steps = count + 3
    extra = FF // D

    def kernel(seq_ref, att_ref, wo_ref, up_ref, shard_ref, part_ref, index_ref, vec_ref, hb_ref, valid_ref,
               full_ref, hid_ref, slope_ref, low_ref, normal_ref, spread_ref, layer_ref, feed_low_ref, sum_ref, sums_ref,
               first, low, normal, hidden, feed, weight, dealt, cot, send, recv, local):
        spot = Spot(groups, depth)
        sems = Sems(send, recv)
        pieces = [GatherPiece(spot, sems, local.at[t], shard_ref.at[t], full_ref.at[t]) for t in range(count)]
        swap = Swap(spot, sems, local.at[count], dealt, cot)
        keep_low = pltpu.make_async_copy(low, low_ref, local.at[count + 1])
        keep_normal = pltpu.make_async_copy(normal, normal_ref, local.at[count + 2])
        keep_hidden = [
            pltpu.make_async_copy(hidden.at[q], hid_ref.at[q], local.at[count + 3 + q]) for q in range(count)
        ]
        keep_sum = pltpu.make_async_copy(feed, sum_ref, local.at[2 * count + 3])
        step = pl.program_id(0)

        @pl.when(step == 0)
        def _():
            greet(everyone(spot))
            reorder(index_ref, part_ref, dealt)

        ticks = Ticks(8)
        starts = [[0, 1, 2, 3], [8, 16, 24, 32], [10, 19, 28, 37], [18, 27, 36, 45], [25, 34, 44, 52]]
        ticks.add_all(timeline(pieces, [[row[q] for row in starts] for q in range(count)]))
        for j, tick in enumerate((3, 5, 8, 9, 10, 11, 16, 17)):
            ticks.add(tick, lambda j=j: swap.start(j, 8))
        chunks = [slice(i, i + ROWS) for i in range(0, span, ROWS)]

        def work(first, last, offset, body):
            @during(first, last)
            def _():
                for c, rows in enumerate(chunks):
                    ticks.here(offset + c, first, last)
                    body(rows)

        def idle(first, last, offset):
            for c in range(len(chunks)):
                ticks.here(offset + c, first, last)

        def norm(rows):
            mixture = seq_ref[rows, :].astype(F32) + product(att_ref[rows, :], wo_ref[...]) + vec_ref[2:3, :]
            centered, spread = normalize(mixture)
            out = centered * vec_ref[6 + extra : 7 + extra, :] + vec_ref[7 + extra : 8 + extra, :]
            first[rows, :] = out
            low[rows, :] = out.astype(BF)
            feed[rows, :] = jnp.broadcast_to(vec_ref[5 + extra : 6 + extra, :], (ROWS, columns))
            normal[rows, :] = centered.astype(BF)
            spread_ref[rows, :] = jnp.broadcast_to(spread, (ROWS, LANES))

        def up(rows):
            q = step - 1
            u = product(low[rows, :], up_ref[0]) + hb_ref[pl.ds(q, 1), :]
            act, slope = gelu_and_slope(u)
            hidden[q, rows, :] = act.astype(BF)
            slope_ref[0, rows, :] = slope.astype(BF)

        def down(rows):
            part = product(hidden[step - 3, rows, :], weight[...].reshape(groups * block, columns))
            feed[rows, :] += part

        work(0, 0, 0, norm)

        @pl.when(step == 0)
        def _():
            keep_low.start()
            keep_normal.start()

        idle(0, 2, 4)
        work(1, count, 0, up)
        for q in range(count):
            pl.when(step == q + 1)(keep_hidden[q].start)
        idle(count + 1, steps - 1, 0)
        for q in range(count):

            @pl.when(step == q + 3)
            def _(q=q):
                ticks.here(4, q + 3, q + 3)
                pltpu.sync_copy(full_ref.at[q], weight)

        @during(3, steps - 1)
        def _():
            for c, rows in enumerate(chunks):
                if c:
                    ticks.here(4 + c, 3, steps - 1)
                down(rows)


        @pl.when(step == steps - 1)
        def _():
            swap.finish()
            sums_ref[...] = jnp.zeros_like(sums_ref)
            pieces_of = span // devices

            def body(rows):
                part = pl.ds(rows.start // pieces_of, ROWS // pieces_of)
                mask = valid_ref[rows, 0:1]
                cotangent = cot[part].reshape(ROWS, columns).astype(F32) * mask
                gain = vec_ref[8 + extra : 9 + extra, :]
                mixture = first[rows, :] + feed[rows, :]
                centered, spread = normalize(mixture)
                layer_ref[rows, :] = ((centered * gain + vec_ref[9 + extra : 10 + extra, :]) * mask).astype(BF)
                back = normalize_back(cotangent, centered, spread, gain)
                back_low = back.astype(BF)
                feed[rows, :] = back
                feed_low_ref[rows, :] = back_low
                sums_ref[0:1, :] += jnp.sum(back_low.astype(F32), axis=0, keepdims=True)
                sums_ref[1:2, :] += jnp.sum(cotangent * centered, axis=0, keepdims=True)
                sums_ref[2:3, :] += jnp.sum(cotangent, axis=0, keepdims=True)

            in_chunks(span, body)
            keep_sum.start()
            keep_low.wait()
            keep_normal.wait()
            for copy in keep_hidden:
                copy.wait()
            keep_sum.wait()

    matrix = lambda kind: jax.ShapeDtypeStruct((span, columns), kind)
    stack = jax.ShapeDtypeStruct((count, span, columns), BF)
    by_q = pl.BlockSpec((1, span, columns), lambda s: (jnp.clip(s - 1, 0, count - 1), 0, 0))
    results = pl.pallas_call(
        kernel,
        grid=(steps,),
        in_specs=[
            still(span, columns), still(span, columns), still(*full_out.shape), by_q, ANYSPEC, still(*parts.shape), SMEMSPEC,
            still(*vectors.shape), still(*hidden_bias.shape), still(*valid.shape),
        ],
        out_specs=[ANYSPEC, ANYSPEC, by_q, ANYSPEC, ANYSPEC]
        + [pl.BlockSpec((span, LANES), lambda s: (0, 0))]
        + [pl.BlockSpec((span, columns), lambda s: (0, 0))] * 2
        + [ANYSPEC, pl.BlockSpec((8, columns), lambda s: (0, 0))],
        out_shape=[
            jax.ShapeDtypeStruct(full_shape(nb, block, columns, count), BF), stack, stack, matrix(BF), matrix(BF),
            jax.ShapeDtypeStruct((span, LANES), F32), matrix(BF), matrix(BF), matrix(F32),
            jax.ShapeDtypeStruct((8, columns), F32),
        ],
        scratch_shapes=[
            pltpu.VMEM((span, columns), F32),
            pltpu.VMEM((span, columns), BF),
            pltpu.VMEM((span, columns), BF),
            pltpu.VMEM((count, span, columns), BF),
            pltpu.VMEM((span, columns), F32),
            pltpu.VMEM(full_shape(nb, block, columns), BF),
            pltpu.VMEM(parts.shape, BF),
            pltpu.VMEM(parts.shape, BF),
            dma(total),
            dma(total),
            dma(2 * count + 4),
        ],
        compiler_params=kernel_params(1),
        name="feed_forward",
    )(sequence, attended, full_out, full_up, shards, parts, index, vectors, hidden_bias, valid)
    return (results[0].reshape(count, groups * block, columns),) + tuple(results[1:])


def feed_backward(mesh, feed_low, low, hidden, slope, full_up, full_down, sum_adjoint, attended, full_out, normal, spread,
                  gain, parts):
    groups, depth = mesh.shape["grp"], mesh.shape["dp"]
    nb = groups // 4
    span, columns = feed_low.shape
    count = hidden.shape[0]
    block, width = columns // groups, columns // depth
    devices = groups * depth
    half = columns // 2
    total = count * reduce_copies(nb, depth) + devices - 1
    work = 3 * count
    steps = work + 2
    boxes = [reduce_boxes(nb, depth, block, columns) for _ in range(count)]
    per = len(boxes[0])

    def kernel(feed_ref, low_ref, hid_ref, slope_ref, up_ref, down_ref, sum_ref, att_ref, wo_ref, normal_ref, spread_ref,
               gain_ref, part_ref,
               change_ref, hb_ref, mix_ref, own_ref, swapped_ref, out_change_ref, att_back_ref, sums_ref,
               back_low, norm, branch, send, recv, local, *box_refs):
        spot = Spot(groups, depth)
        sems = Sems(send, recv)
        tiles = [box_refs[q * per] for q in range(count)]

        def finish(q):
            def store(value):
                own_ref[q] = value

            return store

        pieces = [
            ReducePiece(spot, sems, None, None, width, box_refs[q * per : (q + 1) * per], finish(q)) for q in range(count)
        ]
        swap = Swap(spot, sems, local.at[0], part_ref, swapped_ref)
        keep = pltpu.make_async_copy(norm, mix_ref, local.at[1])
        fetch = pltpu.make_async_copy(sum_ref, norm, local.at[2])
        step = pl.program_id(0)
        ticks = Ticks(4)
        starts = [[3, 7, 11, 15], [7, 19, 27, 35], [17, 25, 33, 41], [22, 30, 38, 46]]
        starts += [[26, 34, 42, 50]] * (len(pieces[0].phases) - 4) + [[31, 39, 47, 54]]
        ticks.add_all(timeline(pieces, [[row[q] for row in starts] for q in range(count)]))
        for j in range(8):
            ticks.add(4 * (j + 2), lambda j=j: swap.start(j, 8))
        chunks = [slice(i, i + ROWS) for i in range(0, span, ROWS)]

        def work_on(first, last, body):
            for c, rows in enumerate(chunks):
                if c == len(chunks) // 2:
                    ticks.here(1, first, last)
                body(rows)
            ticks.here(2, first, last)

        @pl.when(step == 0)
        def _():
            greet(everyone(spot))
            fetch.start()

        ticks.here(0, 0, steps - 1)

        for q in range(count):

            @pl.when(step == q)
            def _(q=q):
                value = product_left(hid_ref[0], feed_ref[...]).astype(BF)
                tiles[q][...] = value.reshape(full_shape(nb, block, columns))

        pl.when(step == count)(fetch.wait)

        for c in (1, 2):
            ticks.here(c, 0, count - 1)

        @during(count, work - 1)
        def _():
            hb_ref[...] = jnp.zeros_like(hb_ref)

            def body(rows):
                value = product_back(feed_ref[rows, :], down_ref[0]) * slope_ref[0, rows, :].astype(F32)
                value = value.astype(BF)
                back_low[rows, :] = value
                hb_ref[0] += jnp.broadcast_to(jnp.sum(value.astype(F32), axis=0, keepdims=True), (8, half))
                norm[rows, :] += product_back(value, up_ref[0])

            work_on(count, work - 1, body)
            change_ref[0] = product_left(low_ref[...], back_low[...]).astype(BF)

        @pl.when(step == work)
        def _():
            sums_ref[...] = jnp.zeros_like(sums_ref)

            def body(rows):
                adjoint = norm[rows, :]
                centered = normal_ref[rows, :].astype(F32)
                back = normalize_back(adjoint, centered, spread_ref[rows, 0:1], gain_ref[6 + count : 7 + count, :])
                back_branch = back.astype(BF)
                norm[rows, :] = back
                branch[rows, :] = back_branch
                sums_ref[0:1, :] += jnp.sum(back_branch.astype(F32), axis=0, keepdims=True)
                sums_ref[1:2, :] += jnp.sum(adjoint * centered, axis=0, keepdims=True)
                sums_ref[2:3, :] += jnp.sum(adjoint, axis=0, keepdims=True)
                att_back_ref[rows, :] = product_back(back_branch, wo_ref[...]).astype(BF)

            work_on(work, work, body)
            keep.start()
            out_change_ref[...] = product_left(att_ref[...], branch[...]).astype(BF)

        ticks.here(3, 0, work)
        for c in range(1, 4):
            ticks.here(c, work + 1, steps - 1)

        @pl.when(step == steps - 1)
        def _():
            keep.wait()
            swap.finish()

    at = lambda s: jnp.clip(s - count, 0, 2 * count - 1)
    by_half = pl.BlockSpec((1, span, half), lambda s: (lax.div(at(s), 2), 0, lax.rem(at(s), 2)))
    whole = lambda *dims: pl.BlockSpec(dims, lambda s: (0,) * len(dims))
    return pl.pallas_call(
        kernel,
        grid=(steps,),
        in_specs=[
            still(span, columns), still(span, columns),
            pl.BlockSpec((1, span, columns), lambda s: (jnp.minimum(s, count - 1), 0, 0)),
            by_half, by_half,
            pl.BlockSpec((1, half, columns), lambda s: (lax.div(at(s), 2), lax.rem(at(s), 2), 0)),
            ANYSPEC, still(span, columns), still(columns, columns), still(span, columns), still(span, LANES),
            still(*gain.shape), ANYSPEC,
        ],
        out_specs=[
            by_half,
            pl.BlockSpec((1, 8, half), lambda s: (lax.div(at(s), 2), 0, lax.rem(at(s), 2))),
            ANYSPEC, whole(count, block, width), ANYSPEC, whole(columns, columns), whole(span, columns), whole(8, columns),
        ],
        out_shape=[
            jax.ShapeDtypeStruct((count, columns, columns), BF),
            jax.ShapeDtypeStruct((count, 8, columns), F32),
            jax.ShapeDtypeStruct((span, columns), F32),
            jax.ShapeDtypeStruct((count, block, width), F32),
            jax.ShapeDtypeStruct(parts.shape, BF),
            jax.ShapeDtypeStruct((columns, columns), BF),
            jax.ShapeDtypeStruct((span, columns), BF),
            jax.ShapeDtypeStruct((8, columns), F32),
        ],
        scratch_shapes=[
            pltpu.VMEM((span, half), BF),
            pltpu.VMEM((span, columns), F32),
            pltpu.VMEM((span, columns), BF),
            dma(total),
            dma(total),
            dma(3),
        ]
        + [box for some in boxes for box in some],
        compiler_params=kernel_params(2),
        name="feed_backward",
    )(feed_low, low, hidden, slope, full_up, full_down, sum_adjoint, attended, full_out, normal, spread, gain, parts)


def attend_back_and_reduce(mesh, projected, query_global, marks, place, attended, attended_adjoint, log_sums, log_sums_global,
                           changes, parts, full_in, sequence, mixture_adjoint, hidden_sums, feed_sums, norm_sums, order):
    groups, depth = mesh.shape["grp"], mesh.shape["dp"]
    nb = groups // 4
    span, columns = sequence.shape
    pairs = H // 2
    count = full_in.shape[0]
    few = query_global.shape[0]
    block, width = columns // groups, columns // depth
    devices = groups * depth
    views = [c.reshape((-1,) + full_shape(nb, block, columns)) for c in changes]
    where = [(i, t) for i, v in enumerate(views) for t in range(v.shape[0])]
    early = len(where)
    given = len(views)
    vec_rows = 16
    extra = hidden_sums.shape[0]
    total = (early + count) * reduce_copies(nb, depth) + devices - 1 + depth - 1 + groups - 1
    late_starts = [4 * (pairs + t) + 1 for t in range(count)]
    fresh = early - early // 2
    steps = (late_starts[-1] + 17) // 4 + 1
    boxes = [reduce_boxes(nb, depth, block, columns) for _ in range(early + fresh)]
    for i in range(count - fresh, early):
        boxes[i][0] = pltpu.VMEM((2, nb, 1, block, columns), BF)
    per = len(boxes[0])

    def kernel(*refs):
        stack_ref, few_ref, marks_ref, place_ref, a_ref, da_ref, lse_ref, lse_global_ref = refs[:8]
        change_refs, refs = refs[8 : 8 + given], refs[8 + given :]
        part_ref, weight_ref, seq_ref, mix_ref, hidden_ref, feed_ref, norm_ref = refs[:7]
        own_refs, own_in_ref, vec_out, grad_ref, swapped_ref = refs[7 : 7 + given], *refs[7 + given : 11 + given]
        refs = refs[11 + given :]
        bias, back, dqg, sums, dk_sum, dv_sum, grad, vec, vec_z, vec_g, send, recv, local, free = refs[:14]
        box_refs = refs[14:]
        spot = Spot(groups, depth)
        sems = Sems(send, recv)

        def finish(ref, i):
            def store(value):
                ref[i] = value

            return store

        box = lambda i: box_refs[i * per : (i + 1) * per]
        pieces = [
            ReducePiece(spot, sems, local.at[i], change_refs[v].at[t], width, box(i), finish(own_refs[v], t))
            for i, (v, t) in enumerate(where)
        ]
        late_box = list(range(early, early + fresh)) + list(range(count - fresh))
        late = [
            ReducePiece(spot, sems, None, None, width, box(late_box[t]), finish(own_in_ref, int(order[t]))) for t in range(count)
        ]
        tiles = [box_refs[late_box[t] * per] for t in range(count)]
        swap = Swap(spot, sems, local.at[early], part_ref, swapped_ref)
        fetch = pltpu.make_async_copy(mix_ref, grad, local.at[early + 1])
        keep = pltpu.make_async_copy(back.at[0], grad_ref, local.at[early + 2])
        part = lambda zz: pl.ds(pl.multiple_of(zz * width, LANES), width)
        first = [
            sems.copy(vec.at[:, part(spot.z_off(i))], vec_z.at[i - 1], spot.at(z=spot.z_off(i)))
            for i in range(1, depth)
        ]
        second = [
            sems.copy(vec_g.at[spot.g], vec_g.at[spot.g], (lax.rem(spot.g + i, groups), spot.z))
            for i in range(1, groups)
        ]
        step = pl.program_id(0)
        ticks = Ticks(4)
        more = len(pieces[0].phases) - 4
        ticks.add_all(
            timeline(
                pieces,
                [
                    [max(0, 6 * t - 4), 6 * t + 2, 6 * t + 12, 6 * t + 22] + [6 * t + 26] * more + [6 * t + 30]
                    for t in range(early)
                ],
            )
        )
        for j in range(4 * pairs - 1):
            ticks.add(1 + j, lambda j=j: swap.start(j, 4 * pairs - 1))

        def freed():
            for target in spot.neighbours():
                pl.semaphore_signal(free, inc=1, device_id=target, device_id_type=MESH)

        ticks.add(6 * (count - fresh - 1) + 30, freed)
        ticks.add(late_starts[fresh], lambda: pl.semaphore_wait(free, len(spot.neighbours())))
        late_times = [[m, m + 2, m + 7, m + 12] + [m + 14] * more + [m + 17] for m in late_starts]
        ticks.add_all(timeline(late, late_times))

        @pl.when(step == 0)
        def _():
            greet(everyone(spot))
            fetch.start()
            make_bias(marks_ref, bias)

        @pl.when(step < pairs)
        def _():
            lanes = pl.ds(pl.multiple_of(step * LANES, LANES), LANES)
            attention_backward(
                [stack_ref.at[i] for i in range(5)], few_ref, bias, marks_ref, place_ref,
                a_ref, da_ref, lse_ref, lse_global_ref,
                [back.at[i, :, lanes] for i in range(5)], dqg.at[:, lanes], sums.at[:, lanes], dk_sum, dv_sum,
                lambda c: ticks.here(c, 0, pairs - 1),
            )

        @pl.when(step == pairs)
        def _():
            fetch.wait()
            vec[...] = jnp.zeros_like(vec)
            vec[0:2, :] = sums[0:2, :]
            vec[2:3, :] = norm_ref[0:1, :]
            vec[3:5, :] = sums[2:4, :]
            vec[5 : 5 + extra, :] = hidden_ref[...]
            vec[5 + extra : 6 + extra, :] = feed_ref[0:1, :]
            vec[6 + extra : 8 + extra, :] = norm_ref[1:3, :]
            vec[8 + extra : 10 + extra, :] = feed_ref[1:3, :]
            start_all(first)

        ticks.here(0, pairs, steps - 1)

        for t in range(count - 1):

            @pl.when(step == pairs + t)
            def _(t=t):
                value = product_left(seq_ref[...], back[t]).astype(BF)
                tiles[t][...] = value.reshape(full_shape(nb, block, columns))

        @pl.when(step == pairs + count - 1)
        def _():
            rows = product_left(place_ref[...], seq_ref[:ROWS, :]).astype(BF)
            value = product_left(rows, dqg[...]).astype(BF)
            tiles[count - 1][...] = value.reshape(full_shape(nb, block, columns))

        ticks.here(1, pairs, steps - 1)

        def grad_rows(first_row, last_row):
            @during(pairs, pairs + count - 2)
            def _():
                for r in range(first_row, last_row, ROWS):
                    rows = slice(r, r + ROWS)
                    grad[rows, :] += product_back(back[step - pairs, rows, :], weight_ref[0])

        grad_rows(0, span // 2)
        ticks.here(2, pairs, steps - 1)
        grad_rows(span // 2, span)

        @pl.when(step == pairs + count - 1)
        def _():
            extra = product_back(dqg[...], weight_ref[0])
            grad[:ROWS, :] += lax.dot_general(
                place_ref[...].astype(F32), extra, (((1,), (0,)), ((), ())),
                precision=lax.Precision.HIGHEST, preferred_element_type=F32,
            )
            back[0] = grad[...].astype(BF)
            keep.start()

        ticks.here(3, pairs, steps - 1)

        @pl.when(step == pairs + 1)
        def _():
            recv_all(first)
            mine = vec[:, part(spot.z)]
            for i in range(depth - 1):
                mine = mine + vec_z[i]
            vec_g[spot.g] = mine
            start_all(second)

        @pl.when(step == steps - 1)
        def _():
            recv_all(second)
            whole = vec_g[0]
            for i in range(1, groups):
                whole = whole + vec_g[i]
            vec_out[...] = whole
            send_done(first)
            send_done(second)
            keep.wait()
            swap.finish()

    at = lambda s: jnp.minimum(s, pairs - 1)
    whole = lambda *dims: pl.BlockSpec(dims, lambda s: (0,) * len(dims))
    column = lambda rows: pl.BlockSpec((rows, LANES), lambda s: (0, at(s)))
    return pl.pallas_call(
        kernel,
        grid=(steps,),
        in_specs=[
            pl.BlockSpec((5, span, LANES), lambda s: (0, 0, at(s))),
            column(few), still(*marks.shape), still(*place.shape), column(span), column(span),
            pl.BlockSpec((1, 8, span), lambda s: (at(s), 0, 0)),
            pl.BlockSpec((1, 8, LANES), lambda s: (at(s), 0, 0)),
        ]
        + [ANYSPEC] * (given + 1)
        + [
            pl.BlockSpec(
                (1, columns, columns), lambda s: (jnp.clip(s - pairs, 0, count - 1), 0, 0), pipeline_mode=pl.Buffered(1)
            ),
            still(span, columns), ANYSPEC, still(*hidden_sums.shape), still(*feed_sums.shape), still(*norm_sums.shape),
        ],
        out_specs=[whole(v.shape[0], block, width) for v in views]
        + [whole(count, block, width), whole(vec_rows, width), ANYSPEC, ANYSPEC],
        out_shape=[jax.ShapeDtypeStruct((v.shape[0], block, width), F32) for v in views]
        + [
            jax.ShapeDtypeStruct((count, block, width), F32),
            jax.ShapeDtypeStruct((vec_rows, width), F32),
            jax.ShapeDtypeStruct((span, columns), BF),
            jax.ShapeDtypeStruct(parts.shape, BF),
        ],
        scratch_shapes=[
            pltpu.VMEM((span, span), F32),
            pltpu.VMEM((5, span, columns), BF),
            pltpu.VMEM((few, columns), BF),
            pltpu.VMEM((8, columns), F32),
            pltpu.VMEM((span, LANES), F32),
            pltpu.VMEM((span, LANES), F32),
            pltpu.VMEM((span, columns), F32),
            pltpu.VMEM((vec_rows, columns), F32),
            pltpu.VMEM((depth - 1, vec_rows, width), F32),
            pltpu.VMEM((groups, vec_rows, width), F32),
            dma(total),
            dma(total),
            dma(early + 3),
            pltpu.SemaphoreType.REGULAR,
        ]
        + [box for some in boxes for box in some],
        compiler_params=kernel_params(3),
        name="attend_back_and_reduce",
    )(projected, query_global, marks, place, attended, attended_adjoint, log_sums, log_sums_global, *views, parts, full_in,
      sequence, mixture_adjoint, hidden_sums, feed_sums, norm_sums)


def up_parts(matrix, ratio, parts):
    rows, columns = matrix.shape
    r = columns // (ratio * parts)
    return matrix.reshape(rows, ratio, parts, r).transpose(2, 0, 1, 3).reshape(parts, rows, ratio * r)


def up_whole(stack, ratio):
    parts, rows, columns = stack.shape
    r = columns // ratio
    return stack.reshape(parts, rows, ratio, r).transpose(1, 2, 0, 3).reshape(rows, parts * columns)


def per_device(mesh, tokens, out_cotangent, lengths, places, deal, in_weights, out_weight, up_weight, down_weight, vectors,
               first_in, first_out, first_up, first_down, first_vectors,
               second_in, second_out, second_up, second_down, second_vectors):
    groups, depth = mesh.shape["grp"], mesh.shape["dp"]
    ratio = groups // depth
    devices = groups * depth
    span = tokens.shape[1]
    quarters = FF // D
    ids = jnp.arange(devices, dtype=jnp.int32)
    inverse = jnp.sum(jnp.where(deal[None, :] == ids[:, None], ids[None, :], 0), axis=1)
    sequence = tokens[0]
    order = np.array([1, 2, 0, 4, 5, 3])

    low_in = jnp.stack([in_weights[i] for i in order]).astype(BF)
    low_rest = jnp.concatenate([out_weight.astype(BF)[None], up_parts(up_weight.astype(BF), ratio, quarters)])
    low_down = down_weight.astype(BF).reshape(quarters, -1, down_weight.shape[1])
    nv = vectors.shape[0]
    low_vectors = jnp.pad(vectors, ((0, 16 - nv), (0, 0))).astype(BF)

    shape_parts = (devices, span // devices, D)

    (full_in, full_out, full_up, _, projected, query_global, attended, log_sums, log_sums_global,
     cotangent_parts, marks, place, vector_rows) = project_and_attend(
        mesh, low_in, low_rest, low_vectors, sequence, places, lengths[:, None], out_cotangent.reshape(shape_parts)
    )
    hidden_bias = vector_rows[5 : 5 + quarters].reshape(groups, quarters, -1).transpose(1, 0, 2).reshape(quarters, D)
    full_down, hidden, slope, first_low, normal_one, spread_one, layer_out, feed_low, sum_adjoint, feed_sums = feed_forward(
        mesh, sequence, attended, full_out, full_up, low_down, cotangent_parts, deal, vector_rows, hidden_bias, marks
    )
    up_change, hidden_sums, mixture_adjoint, part_down, layer_parts, out_change, attended_adjoint, norm_sums = feed_backward(
        mesh, feed_low, first_low, hidden, slope, full_up, full_down, sum_adjoint, attended, full_out, normal_one, spread_one,
        vector_rows, layer_out.reshape(shape_parts)
    )
    layer_parts = layer_parts.at[inverse].get(mode="promise_in_bounds")
    hidden_bias_change = hidden_sums[:, 0].reshape(quarters, groups, -1).transpose(1, 0, 2).reshape(quarters, D)
    part_up, part_out, part_in, part_vectors, token_gradient, layer_mine = attend_back_and_reduce(
        mesh, projected, query_global, marks, place, attended, attended_adjoint, log_sums, log_sums_global,
        (up_change, out_change), layer_parts, full_in, sequence, mixture_adjoint, hidden_bias_change, feed_sums, norm_sums,
        order
    )

    step_count = jnp.float32(STEP)
    fix_first = 1.0 - jnp.power(jnp.float32(BETA_FIRST), step_count)
    fix_second = 1.0 - jnp.power(jnp.float32(BETA_SECOND), step_count)

    def adam(weight, gradient, moment, square, decay):
        return adam_update(weight, gradient, moment, square, decay, fix_first, fix_second)

    part_up = up_whole(part_up, ratio)
    part_out = part_out[0]
    part_down = part_down.reshape(down_weight.shape)
    update_in, moment_in, square_in = adam(in_weights, part_in, first_in, second_in, WEIGHT_DECAY)
    update_out, moment_out, square_out = adam(out_weight, part_out, first_out, second_out, WEIGHT_DECAY)
    update_up, moment_up, square_up = adam(up_weight, part_up, first_up, second_up, WEIGHT_DECAY)
    update_down, moment_down, square_down = adam(down_weight, part_down, first_down, second_down, WEIGHT_DECAY)
    update_vectors, moment_vectors, square_vectors = adam(vectors, part_vectors[:nv], first_vectors, second_vectors, 0.0)
    return (
        layer_mine.reshape(tokens.shape), token_gradient[None],
        update_in, update_out, update_up, update_down, update_vectors,
        moment_in, moment_out, moment_up, moment_down, moment_vectors,
        square_in, square_out, square_up, square_down, square_vectors,
    )


def solution(mesh):
    sequences = P(("grp", "dp"), None, None)
    stack, matrix, rows = P(None, "grp", "dp"), P("grp", "dp"), P(None, "dp")
    packed = (stack, matrix, matrix, matrix, rows)
    return jax.shard_map(
        lambda *arrays: per_device(mesh, *arrays),
        mesh=mesh,
        in_specs=(sequences, sequences, P(), P(), P()) + packed * 3,
        out_specs=(sequences, sequences) + packed * 3,
        check_vma=False,
    )
```
